32 devices in a mesh: slab: 16 (over z, x, core), band: 2 (over y).
Axes of the slice: x: 2, y: 2, z: 4, core: 2. Of those that a mesh axis runs over, the one named last changes fastest.
Arguments:
- hamiltonian: bfloat16 [128, 7, 128, 128], P('slab', None, 'band'), may hold values from -0.1875 to 0.1875
- neighbors: int32 [128, 7], P('slab'), may hold values from 0 to 11, as said below
- orbitals: bfloat16 [16384, 1024], P('slab', 'band'), may hold values from -6 to 6
Outputs:
- residual: bfloat16 [16384, 1024], P(('slab', 'band'))
The draws below stay inside these ranges and needn't reach their ends.
Inputs may be any that keep to these rules, and one draw needn't show every extreme that they name: `neighbors`: window positions 0 to 1 are the last 2 elements of the slab below (periodic), 2 to 9 the slab's own elements, the rest the first 2 elements of the slab above. A slab's elements are in layers of 2; each block row names, in an order of its own, itself, the element 2 positions below and above it in the window, and four elements of its own layer (repeats possible).
All inputs are finite; a program needn't handle non-finite values.
Results may differ from the reference program's by a relative error of at most 0.012.
Values may be sent and summed in bfloat16 or wider, within the bound.
A program may use at most 64 MiB of HBM per device.

```python
import math
import jax
import jax.numpy as jnp

TILE = 128
BANDS = 1024
FACE = 2
BLK_DEV = 8
NBLK = 128
ROWS = 16384


def draw_neighbors(key, part):
    block_index = jnp.arange(NBLK, dtype=jnp.int32)
    within = block_index % BLK_DEV
    layer_base = FACE + within // FACE * FACE
    plane_key = jax.random.fold_in(key, 11)
    order_key = jax.random.fold_in(key, 23)
    inplane = layer_base[:, None] + jax.random.randint(plane_key, (NBLK, 4), 0, FACE, dtype=jnp.int32)
    itself = (FACE + within)[:, None]
    below = within[:, None]
    above = (2 * FACE + within)[:, None]
    columns = jnp.concatenate([itself, below, above, inplane], axis=1).astype(jnp.int32)
    row_keys = jax.random.split(order_key, NBLK)
    orders = jax.vmap(lambda k: jax.random.permutation(k, 7))(row_keys).astype(jnp.int32)
    return jnp.take_along_axis(columns, orders, axis=1).astype(jnp.int32)


def levels(own_key, shape, shards, smallest, largest):
    level, own = 1.0, jax.random.fold_in(own_key, 6)
    for position, blocks in shards:
        heights = jnp.exp(jax.random.uniform(jax.random.fold_in(own, position), (blocks,), jnp.float32, smallest / len(shards), largest / len(shards)))
        level = level * jnp.repeat(heights, shape[position] // blocks).reshape([-1 if axis == position else 1 for axis in range(len(shape))])
    return level


def centred(stream_key, dims, deviation, most, pieces=(), kind=jnp.bfloat16):
    entries = jax.random.normal(stream_key, dims, jnp.float32) * deviation
    if len(pieces) > 0:
        entries = levels(stream_key, dims, pieces, -0.22, 0.18) * entries
    return jnp.clip(entries, min=-most, max=most).astype(kind)


def setup_inputs(seed: int = 0) -> dict:
    key_list = jax.random.split(jax.random.key(seed), 4)
    return {
        "hamiltonian": centred(key_list[0], (NBLK, 7, TILE, TILE), (7 * TILE) ** -0.5, 0.1875, ((0, 16), (2, 2))),
        "neighbors": draw_neighbors(jax.random.fold_in(key_list[3], 71), 0),
        "orbitals": centred(key_list[2], (ROWS, BANDS), 1.0, 6.0, ((0, 16), (1, 2))),
    }


def reference(hamiltonian, neighbors, orbitals):
    nblk = hamiltonian.shape[0]
    tile_size = hamiltonian.shape[2]
    bands_all = orbitals.shape[1]
    block_index = jnp.arange(nblk, dtype=jnp.int32)
    slab_start = block_index // BLK_DEV * BLK_DEV
    global_cols = ((slab_start[:, None] - FACE + neighbors) % nblk).astype(jnp.int32)

    def apply(vector):
        blocks = vector.reshape(nblk, tile_size, bands_all).astype(jnp.float32)
        total = jnp.zeros((nblk, tile_size, bands_all), jnp.float32)
        for slot in range(7):
            total = total + jnp.einsum('rab,rbc->rac', hamiltonian[:, slot].astype(jnp.float32), blocks[global_cols[:, slot]])
        return total.reshape(nblk * tile_size, bands_all)
    first = apply(orbitals).astype(jnp.bfloat16)
    second = (2.0 * apply(first) - orbitals.astype(jnp.float32)).astype(jnp.bfloat16)
    third = (2.0 * apply(second) - first.astype(jnp.float32)).astype(jnp.bfloat16)
    applied = apply(third).astype(jnp.bfloat16)
    gram_scale = 1.0 / math.sqrt(float(nblk * tile_size) * float(bands_all))
    gram_full = (jnp.dot(third.T, applied, preferred_element_type=jnp.float32) * gram_scale).astype(jnp.bfloat16)
    mixed = jnp.dot(third, gram_full, preferred_element_type=jnp.float32)
    return (applied.astype(jnp.float32) - mixed).astype(jnp.bfloat16)
```

```python
import functools
import math

import jax
import jax.numpy as jnp
from jax import lax
from jax.experimental import pallas as pl
from jax.experimental.pallas import tpu as pltpu
from jax.sharding import PartitionSpec as P

FACE = 2
CHUNKS = 2
STREAMS = 2
MESH = pl.DeviceIdType.MESH


def padded(block, sides, width):
    for axis, dim in sides:
        count = lax.axis_size(axis)
        forward = [(i, i + 1) for i in range(count - 1)]
        forward.append((count - 1, 0))
        backward = [(target, source) for source, target in forward]
        low = lax.ppermute(
            lax.slice_in_dim(block, block.shape[dim] - width, None, axis=dim), axis, forward
        )
        high = lax.ppermute(lax.slice_in_dim(block, 0, width, axis=dim), axis, backward)
        block = jnp.concatenate([low, block, high], axis=dim)
    return block


def apply_local(vector, full_tiles, neighbors):
    tile_size = full_tiles.shape[2]
    extended = padded(vector, (("slab", 0),), FACE * tile_size)
    blocks = extended.reshape(-1, tile_size, vector.shape[1])
    picked_blocks = blocks[neighbors]
    product = jnp.einsum(
        "rjab,rjbc->rac", full_tiles, picked_blocks, preferred_element_type=jnp.float32
    )
    return product.reshape(vector.shape[0], vector.shape[1])


def plain_body(hamiltonian, neighbors, orbitals):
    full_tiles = lax.all_gather(hamiltonian, "band", axis=2, tiled=True)
    first = apply_local(orbitals, full_tiles, neighbors).astype(jnp.bfloat16)
    second = (
        2.0 * apply_local(first, full_tiles, neighbors) - orbitals.astype(jnp.float32)
    ).astype(jnp.bfloat16)
    third = (2.0 * apply_local(second, full_tiles, neighbors) - first.astype(jnp.float32)).astype(
        jnp.bfloat16
    )
    applied = apply_local(third, full_tiles, neighbors).astype(jnp.bfloat16)
    rows_all = orbitals.shape[0] * lax.axis_size("slab")
    bands_all = orbitals.shape[1] * lax.axis_size("band")
    gram_scale = 1.0 / math.sqrt(float(rows_all) * float(bands_all))
    strip_third, strip_applied = (
        lax.all_to_all(third, "band", split_axis=0, concat_axis=1, tiled=True),
        lax.all_to_all(applied, "band", split_axis=0, concat_axis=1, tiled=True),
    )
    row_block = lax.psum_scatter(
        jnp.einsum(
            "rb,rc->bc", strip_third, strip_applied, preferred_element_type=jnp.float32
        ).astype(jnp.bfloat16),
        "band",
        scatter_dimension=0,
        tiled=True,
    ).astype(jnp.float32)
    slab_summed = lax.psum(row_block, "slab")
    gram_block = (slab_summed * gram_scale).astype(jnp.bfloat16)
    mixed = jnp.dot(
        strip_third,
        lax.all_gather(gram_block, "band", axis=0, tiled=True),
        preferred_element_type=jnp.float32,
    )
    return (strip_applied.astype(jnp.float32) - mixed).astype(jnp.bfloat16)


def merged_tiles(hamiltonian, neighbors):
    blocks = hamiltonian.shape[0]
    within = jnp.arange(blocks, dtype=jnp.int32)
    layer = FACE + within // FACE * FACE
    sources = (within, layer, layer + 1, within + 2 * FACE)
    merged = []
    for source in sources:
        total = 0.0
        for slot in range(hamiltonian.shape[1]):
            hit = (neighbors[:, slot] == source)[:, None, None]
            total = total + jnp.where(hit, hamiltonian[:, slot].astype(jnp.float32), 0.0)
        merged.append(total.astype(jnp.bfloat16))
    return jnp.concatenate(merged, axis=2)


def flipped(index, bit):
    return index + bit - 2 * bit * lax.rem(lax.div(index, bit), 2)


def kernel(
    slabs, gram_scale, pieces_ref, orbitals_ref, out_ref,
    tiles, ext0, ext1, ext2, ext3, own_applied, strip3, strip4, gram32, gram16, outgoing, incoming,
    local_sem, send_sem, recv_sem,
):
    slab, band = lax.axis_index("slab"), lax.axis_index("band")
    other = 1 - band
    after, before = lax.rem(slab + 1, slabs), lax.rem(slab + slabs - 1, slabs)
    blocks, part, _ = pieces_ref.shape
    tile = 2 * part
    layers = blocks // FACE
    face = FACE * tile
    rows = blocks * tile
    chunks, _, width = ext0.shape
    strip = rows // 2
    groups = 2 * chunks
    ext = [ext0, ext1, ext2, ext3]
    bits = [1 << i for i in range(slabs.bit_length() - 1)]

    barrier = pltpu.get_barrier_semaphore()
    greeted = [{"band": other}, {"slab": after}, {"slab": before}]
    greeted += [{"slab": flipped(slab, bit)} for bit in bits]

    loads = []
    for c in range(chunks):
        load = pltpu.make_async_copy(
            orbitals_ref.at[:, pl.ds(c * width, width)],
            ext0.at[c, pl.ds(face, rows)],
            local_sem.at[c],
        )
        load.start()
        loads.append(load)
    for target in greeted:
        pl.semaphore_signal(barrier, inc=1, device_id=target, device_id_type=MESH)
    pl.semaphore_wait(barrier, len(greeted))

    sent = []

    def send(source, target, device):
        n = len(sent)
        copy = pltpu.make_async_remote_copy(
            src_ref=source, dst_ref=target, send_sem=send_sem.at[n], recv_sem=recv_sem.at[n],
            device_id=device, device_id_type=MESH,
        )
        copy.start()
        sent.append(copy)
        return copy

    def spans(a):
        if a == 0:
            return ((0, 0, tile), (tile, 2 * tile, 3 * tile))
        return ((0, tile, 3 * tile), (3 * tile, 5 * tile, tile))

    order = [1, 2, 0, 3] if layers == 4 else list(range(layers))
    tile_copies = {}
    mine = pl.multiple_of(band * part, part)
    for layer in order:
        tile_copies[layer] = []
        for a in range(FACE):
            for start, place, size in spans(a):
                tile_copies[layer].append(send(
                    pieces_ref.at[layer * FACE + a, :, pl.ds(start, size)],
                    tiles.at[layer, pl.ds(pl.multiple_of(a * tile + mine, part), part), pl.ds(place, size)],
                    {"band": other},
                ))

    def send_halo(k, c, up):
        if up:
            return send(ext[k].at[c, pl.ds(rows, face)], ext[k].at[c, pl.ds(0, face)], {"slab": after})
        return send(
            ext[k].at[c, pl.ds(face, face)], ext[k].at[c, pl.ds(rows + face, face)], {"slab": before}
        )

    halos = {}
    for c in range(chunks):
        loads[c].wait()
        halos[0, c] = [send_halo(0, c, False), send_halo(0, c, True)]

    for layer in order:
        for a in range(FACE):
            for start, place, size in spans(a):
                tiles[layer, pl.ds(pl.multiple_of(a * tile + mine, part), part), place:place + size] = (
                    pieces_ref[layer * FACE + a, :, start:start + size]
                )
            hole = (tile, 5 * tile) if a == 0 else (0, 4 * tile)
            for place in hole:
                tiles[layer, a * tile:(a + 1) * tile, place:place + tile] = jnp.zeros(
                    (tile, tile), jnp.bfloat16
                )

    def apply_layer(k, c, layer):
        product = jnp.dot(
            tiles[layer], ext[k][c, layer * face:(layer + 3) * face, :],
            preferred_element_type=jnp.float32,
        )
        inner = slice((layer + 1) * face, (layer + 2) * face)
        if k == 1 or k == 2:
            product = 2.0 * product - ext[k - 1][c, inner, :].astype(jnp.float32)
        if k < 3:
            ext[k + 1][c, inner, :] = product.astype(jnp.bfloat16)
        else:
            own_applied[c, layer * face:(layer + 1) * face, :] = product.astype(jnp.bfloat16)

    strip_copies = {}
    mine_at = pl.multiple_of(band * strip, strip)
    theirs_at = pl.multiple_of(other * strip, strip)

    def send_strip(which, c, source, base):
        place = strip3 if which == 3 else strip4
        group = band * chunks + c
        strip_copies[which, c] = send(
            source.at[c, pl.ds(base + theirs_at, strip)], place.at[group], {"band": other}
        )
        place[group] = source[c, pl.ds(base + mine_at, strip), :]

    for k in range(4):
        for c in range(chunks):
            inside = list(range(1, layers - 1))
            for layer in inside:
                if k == 0 and c == 0:
                    for copy in tile_copies[layer]:
                        copy.wait_recv()
                apply_layer(k, c, layer)
            for layer, halo in ((0, 1), (layers - 1, 0)):
                if k == 0 and c == 0:
                    for copy in tile_copies[layer]:
                        copy.wait_recv()
                halos[k, c][halo].wait_recv()
                apply_layer(k, c, layer)
                if k < 3:
                    halos.setdefault((k + 1, c), []).append(send_halo(k + 1, c, layer != 0))
            if k == 2:
                send_strip(3, c, ext3, face)
            if k == 3:
                send_strip(4, c, own_applied, 0)

    def gram_block(p, q):
        at = pl.multiple_of((p * groups + q) * width, width)
        gram32[pl.ds(at, width), :] = lax.dot_general(
            strip3[p], strip4[q], (((0,), (0,)), ((), ())), preferred_element_type=jnp.float32
        )

    for c in range(chunks):
        for d in range(chunks):
            gram_block(band * chunks + d, band * chunks + c)
    for c in range(chunks):
        strip_copies[3, c].wait_recv()
    for c in range(chunks):
        for d in range(chunks):
            gram_block(other * chunks + d, band * chunks + c)
    for c in range(chunks):
        strip_copies[4, c].wait_recv()
        for p in range(groups):
            gram_block(p, other * chunks + c)

    near, far = bits[0], bits[1:]
    routes = [
        [("slab", far[0]), ("band", 1)] + [("slab", b) for b in far[1:]],
        [("band", 1), ("slab", far[0])] + [("slab", b) for b in far[:0:-1]],
    ]

    def side_and_target(axis, bit):
        at = slab if axis == "slab" else band
        return lax.rem(lax.div(at, bit), 2), {axis: flipped(at, bit)}

    total = gram32.shape[0]
    used = [0]

    def send_half(from_at, length, target):
        start = used[0]
        used[0] += length
        outgoing[start:start + length, :] = gram32[pl.ds(from_at, length), :].astype(jnp.bfloat16)
        copy = send(outgoing.at[pl.ds(start, length)], incoming.at[pl.ds(start, length)], target)
        return copy, start

    def add_half(pending, keep, length):
        copy, start = pending
        copy.wait_recv()
        gram32[pl.ds(keep, length), :] += incoming[start:start + length, :].astype(jnp.float32)

    side, target = side_and_target("slab", near)
    piece = total // 2 // STREAMS
    state = []
    for s in range(STREAMS):
        there = pl.multiple_of((1 - side) * (total // 2) + s * piece, piece)
        here = pl.multiple_of(side * (total // 2) + s * piece, piece)
        state.append([send_half(there, piece, target), here, piece])
    trail = [[] for _ in range(STREAMS)]
    for step in range(len(routes[0])):
        for s in range(STREAMS):
            pending, here, length = state[s]
            add_half(pending, here, length)
            axis, bit = routes[s][step]
            side, target = side_and_target(axis, bit)
            half = length // 2
            trail[s].append((here, length, target))
            keep = pl.multiple_of(here + side * half, half)
            away = pl.multiple_of(here + (1 - side) * half, half)
            state[s] = [send_half(away, half, target), keep, half]
    side, target = side_and_target("slab", near)
    back = []
    for s in range(STREAMS):
        pending, here, length = state[s]
        add_half(pending, here, length)
        gram16[pl.ds(here, length), :] = (gram32[pl.ds(here, length), :] * gram_scale).astype(
            jnp.bfloat16
        )
        back.append([None, here, length])
    for step in range(len(routes[0]) + 1):
        for s in range(STREAMS):
            copy, here, length = back[s]
            if copy is not None:
                copy.wait_recv()
                here, length, _ = trail[s][len(routes[0]) - step]
            to = trail[s][len(routes[0]) - 1 - step][2] if step < len(routes[0]) else target
            part_ref = gram16.at[pl.ds(here, length)]
            back[s] = [send(part_ref, part_ref, to), here, length]
    for s in range(STREAMS):
        back[s][0].wait_recv()

    for q in range(groups):
        mixed = jnp.zeros((strip, width), jnp.float32)
        for p in range(groups):
            at = (p * groups + q) * width
            mixed += jnp.dot(
                strip3[p], gram16[at:at + width, :], preferred_element_type=jnp.float32
            )
        out_ref[:, q * width:(q + 1) * width] = (
            strip4[q].astype(jnp.float32) - mixed
        ).astype(jnp.bfloat16)
    for copy in sent:
        copy.wait_send()


def fused_body(slabs, hamiltonian, neighbors, orbitals):
    blocks, _, part, tile = hamiltonian.shape
    rows, bands = orbitals.shape
    layers = blocks // FACE
    width = bands // CHUNKS
    groups = 2 * CHUNKS
    strip = rows // 2
    face = FACE * tile
    total = groups * groups * width
    gram_scale = 1.0 / math.sqrt(float(rows * slabs) * float(bands * 2))
    steps = slabs.bit_length()
    copies = 4 * blocks // 2 + 8 * CHUNKS + 2 * CHUNKS + 2 * STREAMS * steps
    half = jnp.bfloat16
    pieces = merged_tiles(hamiltonian, neighbors)
    flops = 2 * rows * 6 * tile * bands * 4 + 2 * 2 * strip * 4 * bands * bands
    return pl.pallas_call(
        functools.partial(kernel, slabs, gram_scale),
        out_shape=jax.ShapeDtypeStruct((strip, 2 * bands), half),
        in_specs=[pl.BlockSpec(memory_space=pltpu.VMEM), pl.BlockSpec(memory_space=pl.ANY)],
        out_specs=pl.BlockSpec(memory_space=pltpu.VMEM),
        scratch_shapes=[
            pltpu.VMEM((layers, face, 3 * face), half),
            *[pltpu.VMEM((CHUNKS, rows + 2 * face, width), half) for _ in range(4)],
            pltpu.VMEM((CHUNKS, rows, width), half),
            pltpu.VMEM((groups, strip, width), half),
            pltpu.VMEM((groups, strip, width), half),
            pltpu.VMEM((total, width), jnp.float32),
            pltpu.VMEM((total, width), half),
            pltpu.VMEM((total, width), half),
            pltpu.VMEM((total, width), half),
            pltpu.SemaphoreType.DMA((CHUNKS,)),
            pltpu.SemaphoreType.DMA((copies,)),
            pltpu.SemaphoreType.DMA((copies,)),
        ],
        compiler_params=pltpu.CompilerParams(
            collective_id=0, has_side_effects=True, vmem_limit_bytes=48 * 1024 * 1024
        ),
        cost_estimate=pl.CostEstimate(flops=flops, bytes_accessed=4 * rows * bands, transcendentals=0),
    )(pieces, orbitals)


def solution(mesh):
    in_specs = (P("slab", None, "band", None), P("slab", None), P("slab", "band"))
    out_specs = P(("slab", "band"), None)
    slabs, groups = mesh.shape["slab"], mesh.shape["band"]
    pairs = groups == 2 and slabs >= 8 and slabs & (slabs - 1) == 0
    body = functools.partial(fused_body, slabs) if pairs else plain_body
    return jax.shard_map(body, mesh=mesh, in_specs=in_specs, out_specs=out_specs, check_vma=False)
```

```python
import functools
import math

import jax
import jax.numpy as jnp
from jax import lax
from jax.experimental import pallas as pl
from jax.experimental.pallas import tpu as pltpu
from jax.sharding import PartitionSpec as P

FACE = 2
CHUNKS = 2
MESH = pl.DeviceIdType.MESH


def padded(block, sides, width):
    for axis, dim in sides:
        count = lax.axis_size(axis)
        forward = [(i, i + 1) for i in range(count - 1)]
        forward.append((count - 1, 0))
        backward = [(target, source) for source, target in forward]
        low = lax.ppermute(
            lax.slice_in_dim(block, block.shape[dim] - width, None, axis=dim), axis, forward
        )
        high = lax.ppermute(lax.slice_in_dim(block, 0, width, axis=dim), axis, backward)
        block = jnp.concatenate([low, block, high], axis=dim)
    return block


def apply_local(vector, full_tiles, neighbors):
    tile_size = full_tiles.shape[2]
    extended = padded(vector, (("slab", 0),), FACE * tile_size)
    blocks = extended.reshape(-1, tile_size, vector.shape[1])
    picked_blocks = blocks[neighbors]
    product = jnp.einsum(
        "rjab,rjbc->rac", full_tiles, picked_blocks, preferred_element_type=jnp.float32
    )
    return product.reshape(vector.shape[0], vector.shape[1])


def plain_body(hamiltonian, neighbors, orbitals):
    full_tiles = lax.all_gather(hamiltonian, "band", axis=2, tiled=True)
    first = apply_local(orbitals, full_tiles, neighbors).astype(jnp.bfloat16)
    second = (
        2.0 * apply_local(first, full_tiles, neighbors) - orbitals.astype(jnp.float32)
    ).astype(jnp.bfloat16)
    third = (2.0 * apply_local(second, full_tiles, neighbors) - first.astype(jnp.float32)).astype(
        jnp.bfloat16
    )
    applied = apply_local(third, full_tiles, neighbors).astype(jnp.bfloat16)
    rows_all = orbitals.shape[0] * lax.axis_size("slab")
    bands_all = orbitals.shape[1] * lax.axis_size("band")
    gram_scale = 1.0 / math.sqrt(float(rows_all) * float(bands_all))
    strip_third, strip_applied = (
        lax.all_to_all(third, "band", split_axis=0, concat_axis=1, tiled=True),
        lax.all_to_all(applied, "band", split_axis=0, concat_axis=1, tiled=True),
    )
    row_block = lax.psum_scatter(
        jnp.einsum(
            "rb,rc->bc", strip_third, strip_applied, preferred_element_type=jnp.float32
        ).astype(jnp.bfloat16),
        "band",
        scatter_dimension=0,
        tiled=True,
    ).astype(jnp.float32)
    slab_summed = lax.psum(row_block, "slab")
    gram_block = (slab_summed * gram_scale).astype(jnp.bfloat16)
    mixed = jnp.dot(
        strip_third,
        lax.all_gather(gram_block, "band", axis=0, tiled=True),
        preferred_element_type=jnp.float32,
    )
    return (strip_applied.astype(jnp.float32) - mixed).astype(jnp.bfloat16)


def merged_tiles(hamiltonian, neighbors):
    blocks = hamiltonian.shape[0]
    within = jnp.arange(blocks, dtype=jnp.int32)
    layer = FACE + within // FACE * FACE
    sources = (within, layer, layer + 1, within + 2 * FACE)
    merged = []
    for source in sources:
        total = 0.0
        for slot in range(hamiltonian.shape[1]):
            hit = (neighbors[:, slot] == source)[:, None, None]
            total = total + jnp.where(hit, hamiltonian[:, slot].astype(jnp.float32), 0.0)
        merged.append(total.astype(jnp.bfloat16))
    return jnp.concatenate(merged, axis=2)


def kernel(
    slabs, gram_scale, pieces_ref, orbitals_ref, out_ref,
    tiles, ext0, ext1, ext2, ext3, own_applied, strip3, strip4, own32, to_core, from_core,
    to_peers, from_peers, gram16, out32, local_sem, send_sem, recv_sem,
):
    slab, band = lax.axis_index("slab"), lax.axis_index("band")
    other = 1 - band
    after, before = lax.rem(slab + 1, slabs), lax.rem(slab + slabs - 1, slabs)
    blocks, part, _ = pieces_ref.shape
    tile = 2 * part
    layers = blocks // FACE
    face = FACE * tile
    rows = blocks * tile
    chunks, _, width = ext0.shape
    strip = rows // 2
    groups = 2 * chunks
    ext = [ext0, ext1, ext2, ext3]

    chips, depth = slabs // 2, slabs // 4
    core, chip = lax.rem(slab, 2), lax.div(slab, 2)
    column, level = lax.rem(chip, 2), lax.div(chip, 2)
    sibling = {"slab": chip * 2 + (1 - core)}
    piece = width // chips

    def at_chip(index, plane):
        return {"slab": index * 2 + core, "band": plane}

    def ring(offset):
        return lax.rem(chip + offset, chips)

    barrier = pltpu.get_barrier_semaphore()
    greeted = [{"slab": after}, {"slab": before}, sibling]
    greeted += [at_chip(ring(j), band) for j in range(1, chips)]
    greeted += [at_chip(ring(j), other) for j in range(chips)]

    loads = []
    for c in range(chunks):
        load = pltpu.make_async_copy(
            orbitals_ref.at[:, pl.ds(c * width, width)],
            ext0.at[c, pl.ds(face, rows)],
            local_sem.at[c],
        )
        load.start()
        loads.append(load)
    for target in greeted:
        pl.semaphore_signal(barrier, inc=1, device_id=target, device_id_type=MESH)
    pl.semaphore_wait(barrier, len(greeted))

    sent = []

    def send(source, target, device):
        n = len(sent)
        copy = pltpu.make_async_remote_copy(
            src_ref=source, dst_ref=target, send_sem=send_sem.at[n], recv_sem=recv_sem.at[n],
            device_id=device, device_id_type=MESH,
        )
        copy.start()
        sent.append(copy)
        return copy

    def spans(a):
        if a == 0:
            return ((0, 0, tile), (tile, 2 * tile, 3 * tile))
        return ((0, tile, 3 * tile), (3 * tile, 5 * tile, tile))

    outer = [0, layers - 1]
    inner_layers = list(range(1, layers - 1))
    order = outer + inner_layers
    tile_copies = {}
    mine = pl.multiple_of(band * part, part)
    for layer in order:
        tile_copies[layer] = []
        for a in range(FACE):
            for start, place, size in spans(a):
                tile_copies[layer].append(send(
                    pieces_ref.at[layer * FACE + a, :, pl.ds(start, size)],
                    tiles.at[layer, pl.ds(pl.multiple_of(a * tile + mine, part), part), pl.ds(place, size)],
                    {"band": other},
                ))

    def send_halo(k, c, up):
        if up:
            return send(ext[k].at[c, pl.ds(rows, face)], ext[k].at[c, pl.ds(0, face)], {"slab": after})
        return send(
            ext[k].at[c, pl.ds(face, face)], ext[k].at[c, pl.ds(rows + face, face)], {"slab": before}
        )

    halos = {}
    for c in range(chunks):
        loads[c].wait()
        halos[0, c] = [send_halo(0, c, False), send_halo(0, c, True)]

    for layer in order:
        for a in range(FACE):
            for start, place, size in spans(a):
                tiles[layer, pl.ds(pl.multiple_of(a * tile + mine, part), part), place:place + size] = (
                    pieces_ref[layer * FACE + a, :, start:start + size]
                )
            hole = (tile, 5 * tile) if a == 0 else (0, 4 * tile)
            for place in hole:
                tiles[layer, a * tile:(a + 1) * tile, place:place + tile] = jnp.zeros(
                    (tile, tile), jnp.bfloat16
                )

    def apply_layer(k, c, layer):
        product = jnp.dot(
            tiles[layer], ext[k][c, layer * face:(layer + 3) * face, :],
            preferred_element_type=jnp.float32,
        )
        inner = slice((layer + 1) * face, (layer + 2) * face)
        if k == 1 or k == 2:
            product = 2.0 * product - ext[k - 1][c, inner, :].astype(jnp.float32)
        if k < 3:
            ext[k + 1][c, inner, :] = product.astype(jnp.bfloat16)
        else:
            own_applied[c, layer * face:(layer + 1) * face, :] = product.astype(jnp.bfloat16)

    strip_copies = {}
    mine_at = pl.multiple_of(band * strip, strip)
    theirs_at = pl.multiple_of(other * strip, strip)

    def send_strip(which, c, source, base):
        place = strip3 if which == 3 else strip4
        group = band * chunks + c
        strip_copies[which, c] = send(
            source.at[c, pl.ds(base + theirs_at, strip)], place.at[group], {"band": other}
        )
        place[group] = source[c, pl.ds(base + mine_at, strip), :]

    def outer_layer(k, c, layer):
        halos[k, c][1 if layer == 0 else 0].wait_recv()
        apply_layer(k, c, layer)
        if k < 3:
            halos.setdefault((k + 1, c), []).append(send_halo(k + 1, c, layer != 0))

    for layer in outer:
        for copy in tile_copies[layer]:
            copy.wait_recv()
        for c in range(chunks):
            outer_layer(0, c, layer)
    for layer in inner_layers:
        for copy in tile_copies[layer]:
            copy.wait_recv()
        for c in range(chunks):
            apply_layer(0, c, layer)
    for k in range(1, 4):
        for c in range(chunks):
            for layer in inner_layers:
                apply_layer(k, c, layer)
            for layer in outer:
                outer_layer(k, c, layer)
            if k == 2:
                send_strip(3, c, ext3, face)
            if k == 3:
                send_strip(4, c, own_applied, 0)

    def transposed_dot(left, right):
        return lax.dot_general(
            left, right, (((0,), (0,)), ((), ())), preferred_element_type=jnp.float32
        )

    def unit_start(unit, left, right):
        to_core[unit] = transposed_dot(left(1 - core), right).astype(jnp.bfloat16)
        copy = send(to_core.at[unit], from_core.at[unit], sibling)
        own32[unit] = transposed_dot(left(core), right)
        return copy

    def unit_spread(unit, copy, place, first, plane):
        copy.wait_recv()
        to_peers[unit] = (own32[unit] + from_core[unit].astype(jnp.float32)).astype(jnp.bfloat16)
        copies = []
        for j in range(first, chips):
            target = ring(j)
            copies.append(send(
                to_peers.at[unit, pl.ds(pl.multiple_of(target * piece, piece), piece)],
                from_peers.at[place + j],
                at_chip(target, plane),
            ))
        return copies

    my_piece = pl.multiple_of(chip * piece, piece)

    def summed(unit, places, quad, c):
        total = to_peers[unit, pl.ds(my_piece, piece), :].astype(jnp.float32)
        for place in places:
            total = total + from_peers[place].astype(jnp.float32)
        row = pl.multiple_of(core * width + my_piece, piece)
        gram16[quad * chunks + c, pl.ds(row, piece), :] = (total * gram_scale).astype(jnp.bfloat16)

    def pass_on(quad, index, device):
        row = pl.multiple_of(core * width + index * piece, piece)
        ref = gram16.at[pl.ds(quad * chunks, chunks), pl.ds(row, piece)]
        return send(ref, ref, device)

    def place_of(c, kind):
        return (c * 3 + kind) * chips

    diag = [c for c in range(chunks)]
    near = [chunks + c for c in range(chunks)]
    cross = [2 * chunks + c for c in range(chunks)]

    starts = [
        unit_start(diag[c], lambda d: ext3[d, face:face + rows, :], own_applied[c])
        for c in range(chunks)
    ]
    diag_pieces = [
        unit_spread(diag[c], starts[c], place_of(c, 0), 1, band) for c in range(chunks)
    ]
    for c in range(chunks):
        strip_copies[3, c].wait_recv()
    starts = [
        unit_start(near[c], lambda d: strip3[other * chunks + d], strip4[band * chunks + c])
        for c in range(chunks)
    ]
    near_pieces = [
        unit_spread(near[c], starts[c], place_of(c, 1), 1, band) for c in range(chunks)
    ]

    def level_chip(offset):
        return lax.rem(level + offset, depth) * 2 + column

    own_diag, other_diag = band * 3, other * 3
    for c in range(chunks):
        for copy in diag_pieces[c]:
            copy.wait_recv()
        summed(diag[c], [place_of(c, 0) + j for j in range(1, chips)], own_diag, c)
    across = pass_on(own_diag, chip, at_chip(chip, other))
    beside = level * 2 + (1 - column)
    side_copies, level_copies = [], []

    def spread_level(quad):
        side_copies.append(pass_on(quad, chip, at_chip(beside, band)))
        for j in range(1, depth):
            level_copies.append((quad, j, pass_on(quad, chip, at_chip(level_chip(j), band))))

    spread_level(own_diag)
    across.wait_recv()
    spread_level(other_diag)

    def cross_unit(c):
        strip_copies[4, c].wait_recv()
        start = unit_start(cross[c], lambda d: strip3[band * chunks + d], strip4[other * chunks + c])
        return unit_spread(cross[c], start, place_of(c, 2), 0, other)

    cross_pieces = [cross_unit(0)]
    for quad, j, copy in level_copies:
        copy.wait_recv()
        side_copies.append(pass_on(quad, level_chip(depth - j), at_chip(beside, band)))
    for c in range(1, chunks):
        cross_pieces.append(cross_unit(c))
    for copy in side_copies:
        copy.wait_recv()

    def send_to_sibling(quad):
        row = pl.multiple_of(core * width, width)
        ref = gram16.at[pl.ds(quad * chunks, chunks), pl.ds(row, width)]
        return send(ref, ref, sibling)

    core_copies = [send_to_sibling(own_diag), send_to_sibling(other_diag)]

    own_off, other_off = other * 2 + band, band * 2 + other
    for c in range(chunks):
        for copy in near_pieces[c] + cross_pieces[c]:
            copy.wait_recv()
        places = [place_of(c, 1) + j for j in range(1, chips)]
        places += [place_of(c, 2) + j for j in range(chips)]
        summed(near[c], places, own_off, c)
    plane_copies = []

    def spread_plane(index):
        plane_copies.append((index, [
            pass_on(own_off, index, at_chip(chip, other)),
            pass_on(own_off, index, at_chip(beside, band)),
            pass_on(own_off, index, at_chip(beside, other)),
        ]))

    level_copies = [
        (j, pass_on(own_off, chip, at_chip(level_chip(j), band))) for j in range(1, depth)
    ]
    spread_plane(chip)
    core_copies.append(pass_on(own_off, chip, sibling))
    for j, copy in level_copies:
        copy.wait_recv()
        index = level_chip(depth - j)
        spread_plane(index)
        core_copies.append(pass_on(own_off, index, sibling))
    for copy in core_copies[:2]:
        copy.wait_recv()

    def mix(gr, gc, c):
        block = gram16[(gr * 2 + gc) * chunks + c]
        total = jnp.zeros((strip, width), jnp.float32)
        for d in range(chunks):
            total += jnp.dot(
                strip3[gr * chunks + d], block[d * width:(d + 1) * width],
                preferred_element_type=jnp.float32,
            )
        return total

    for gc in range(2):
        for c in range(chunks):
            q = gc * chunks + c
            out32[q] = strip4[q].astype(jnp.float32) - mix(gc, gc, c)
    for index, (over, aside, corner) in plane_copies:
        apart = index + 1 - 2 * column
        over.wait_recv()
        core_copies.append(pass_on(other_off, index, sibling))
        aside.wait_recv()
        core_copies.append(pass_on(own_off, apart, sibling))
        corner.wait_recv()
        core_copies.append(pass_on(other_off, apart, sibling))
    for copy in core_copies[2:]:
        copy.wait_recv()
    for gc in range(2):
        for c in range(chunks):
            q = gc * chunks + c
            out_ref[:, q * width:(q + 1) * width] = (out32[q] - mix(1 - gc, gc, c)).astype(
                jnp.bfloat16
            )
    for copy in sent:
        copy.wait_send()


def fused_body(slabs, hamiltonian, neighbors, orbitals):
    blocks, _, part, tile = hamiltonian.shape
    rows, bands = orbitals.shape
    layers = blocks // FACE
    width = bands // CHUNKS
    groups = 2 * CHUNKS
    strip = rows // 2
    face = FACE * tile
    chips, depth = slabs // 2, slabs // 4
    piece = width // chips
    units = 3 * CHUNKS
    gram_scale = 1.0 / math.sqrt(float(rows * slabs) * float(bands * 2))
    copies = 2 * blocks + 8 * CHUNKS + 2 * CHUNKS + units * (chips + 1) + 4 * depth + 5
    copies += 4 * depth + 4 * depth + 4
    half = jnp.bfloat16
    pieces = merged_tiles(hamiltonian, neighbors)
    flops = 2 * rows * 6 * tile * bands * 4 + 2 * 2 * strip * 4 * bands * bands
    return pl.pallas_call(
        functools.partial(kernel, slabs, gram_scale),
        out_shape=jax.ShapeDtypeStruct((strip, 2 * bands), half),
        in_specs=[pl.BlockSpec(memory_space=pltpu.VMEM), pl.BlockSpec(memory_space=pl.ANY)],
        out_specs=pl.BlockSpec(memory_space=pltpu.VMEM),
        scratch_shapes=[
            pltpu.VMEM((layers, face, 3 * face), half),
            *[pltpu.VMEM((CHUNKS, rows + 2 * face, width), half) for _ in range(4)],
            pltpu.VMEM((CHUNKS, rows, width), half),
            pltpu.VMEM((groups, strip, width), half),
            pltpu.VMEM((groups, strip, width), half),
            pltpu.VMEM((units, width, width), jnp.float32),
            pltpu.VMEM((units, width, width), half),
            pltpu.VMEM((units, width, width), half),
            pltpu.VMEM((units, width, width), half),
            pltpu.VMEM((units * chips, piece, width), half),
            pltpu.VMEM((4 * CHUNKS, CHUNKS * width, width), half),
            pltpu.VMEM((groups, strip, width), jnp.float32),
            pltpu.SemaphoreType.DMA((CHUNKS,)),
            pltpu.SemaphoreType.DMA((copies,)),
            pltpu.SemaphoreType.DMA((copies,)),
        ],
        compiler_params=pltpu.CompilerParams(
            collective_id=0, has_side_effects=True, vmem_limit_bytes=48 * 1024 * 1024
        ),
        cost_estimate=pl.CostEstimate(flops=flops, bytes_accessed=4 * rows * bands, transcendentals=0),
    )(pieces, orbitals)


def solution(mesh):
    in_specs = (P("slab", None, "band", None), P("slab", None), P("slab", "band"))
    out_specs = P(("slab", "band"), None)
    slabs, groups = mesh.shape["slab"], mesh.shape["band"]
    pairs = groups == 2 and slabs >= 8 and slabs % 4 == 0 and CHUNKS == 2
    body = functools.partial(fused_body, slabs) if pairs else plain_body
    return jax.shard_map(body, mesh=mesh, in_specs=in_specs, out_specs=out_specs, check_vma=False)
```

```python
import functools
import math

import jax
import jax.numpy as jnp
from jax import lax
from jax.experimental import pallas as pl
from jax.experimental.pallas import tpu as pltpu
from jax.sharding import PartitionSpec as P

FACE = 2
CHUNKS = 2
MESH = pl.DeviceIdType.MESH


def padded(block, sides, width):
    for axis, dim in sides:
        count = lax.axis_size(axis)
        forward = [(i, i + 1) for i in range(count - 1)]
        forward.append((count - 1, 0))
        backward = [(target, source) for source, target in forward]
        low = lax.ppermute(
            lax.slice_in_dim(block, block.shape[dim] - width, None, axis=dim), axis, forward
        )
        high = lax.ppermute(lax.slice_in_dim(block, 0, width, axis=dim), axis, backward)
        block = jnp.concatenate([low, block, high], axis=dim)
    return block


def apply_local(vector, full_tiles, neighbors):
    tile_size = full_tiles.shape[2]
    extended = padded(vector, (("slab", 0),), FACE * tile_size)
    blocks = extended.reshape(-1, tile_size, vector.shape[1])
    picked_blocks = blocks[neighbors]
    product = jnp.einsum(
        "rjab,rjbc->rac", full_tiles, picked_blocks, preferred_element_type=jnp.float32
    )
    return product.reshape(vector.shape[0], vector.shape[1])


def plain_body(hamiltonian, neighbors, orbitals):
    full_tiles = lax.all_gather(hamiltonian, "band", axis=2, tiled=True)
    first = apply_local(orbitals, full_tiles, neighbors).astype(jnp.bfloat16)
    second = (
        2.0 * apply_local(first, full_tiles, neighbors) - orbitals.astype(jnp.float32)
    ).astype(jnp.bfloat16)
    third = (2.0 * apply_local(second, full_tiles, neighbors) - first.astype(jnp.float32)).astype(
        jnp.bfloat16
    )
    applied = apply_local(third, full_tiles, neighbors).astype(jnp.bfloat16)
    rows_all = orbitals.shape[0] * lax.axis_size("slab")
    bands_all = orbitals.shape[1] * lax.axis_size("band")
    gram_scale = 1.0 / math.sqrt(float(rows_all) * float(bands_all))
    strip_third, strip_applied = (
        lax.all_to_all(third, "band", split_axis=0, concat_axis=1, tiled=True),
        lax.all_to_all(applied, "band", split_axis=0, concat_axis=1, tiled=True),
    )
    row_block = lax.psum_scatter(
        jnp.einsum(
            "rb,rc->bc", strip_third, strip_applied, preferred_element_type=jnp.float32
        ).astype(jnp.bfloat16),
        "band",
        scatter_dimension=0,
        tiled=True,
    ).astype(jnp.float32)
    slab_summed = lax.psum(row_block, "slab")
    gram_block = (slab_summed * gram_scale).astype(jnp.bfloat16)
    mixed = jnp.dot(
        strip_third,
        lax.all_gather(gram_block, "band", axis=0, tiled=True),
        preferred_element_type=jnp.float32,
    )
    return (strip_applied.astype(jnp.float32) - mixed).astype(jnp.bfloat16)


def kernel(
    slabs, gram_scale, neighbors_ref, hamiltonian_ref, orbitals_ref, out_ref,
    slots, pieces, tiles, ext0, ext1, ext2, ext3, own_applied, strip3, strip4, own32, to_core, from_core,
    to_peers, from_peers, gram16, out32, local_sem, send_sem, recv_sem,
):
    slab, band = lax.axis_index("slab"), lax.axis_index("band")
    other = 1 - band
    after, before = lax.rem(slab + 1, slabs), lax.rem(slab + slabs - 1, slabs)
    blocks, _, part, _ = slots.shape
    tile = 2 * part
    layers = blocks // FACE
    face = FACE * tile
    rows = blocks * tile
    chunks, _, width = ext0.shape
    strip = rows // 2
    groups = 2 * chunks
    ext = [ext0, ext1, ext2, ext3]

    chips, depth = slabs // 2, slabs // 4
    core, chip = lax.rem(slab, 2), lax.div(slab, 2)
    column, level = lax.rem(chip, 2), lax.div(chip, 2)
    sibling = {"slab": chip * 2 + (1 - core)}
    piece = width // chips

    def at_chip(index, plane):
        return {"slab": index * 2 + core, "band": plane}

    def ring(offset):
        return lax.rem(chip + offset, chips)

    barrier = pltpu.get_barrier_semaphore()
    greeted = [{"slab": after}, {"slab": before}, sibling]
    greeted += [at_chip(ring(j), band) for j in range(1, chips)]
    greeted += [at_chip(ring(j), other) for j in range(chips)]

    outer = [0, layers - 1]
    inner_layers = list(range(1, layers - 1))
    order = outer + inner_layers
    tile_loads = {}
    for layer in order:
        span = pl.ds(layer * FACE, FACE)
        tile_loads[layer] = pltpu.make_async_copy(
            hamiltonian_ref.at[span], slots.at[span], local_sem.at[chunks + layer]
        )
        tile_loads[layer].start()
    loads = []
    for c in range(chunks):
        load = pltpu.make_async_copy(
            orbitals_ref.at[:, pl.ds(c * width, width)],
            ext0.at[c, pl.ds(face, rows)],
            local_sem.at[c],
        )
        load.start()
        loads.append(load)
    for target in greeted:
        pl.semaphore_signal(barrier, inc=1, device_id=target, device_id_type=MESH)

    def spans(a):
        if a == 0:
            return ((0, 0, tile), (tile, 2 * tile, 3 * tile))
        return ((0, tile, 3 * tile), (3 * tile, 5 * tile, tile))

    mine = pl.multiple_of(band * part, part)

    def merge(layer):
        tile_loads[layer].wait()
        for a in range(FACE):
            row = layer * FACE + a
            sources = (row, FACE + layer * FACE, FACE + layer * FACE + 1, row + 2 * FACE)
            totals = [jnp.zeros((part, tile), jnp.float32) for _ in sources]
            for slot in range(slots.shape[1]):
                name = neighbors_ref[row, slot]
                entry = slots[row, slot].astype(jnp.float32)
                for n, source in enumerate(sources):
                    totals[n] = totals[n] + jnp.where(name == source, entry, 0.0)
            merged = jnp.concatenate([total.astype(jnp.bfloat16) for total in totals], axis=1)
            pieces[row] = merged
            for start, place, size in spans(a):
                tiles[layer, pl.ds(pl.multiple_of(a * tile + mine, part), part), place:place + size] = (
                    merged[:, start:start + size]
                )
            hole = (tile, 5 * tile) if a == 0 else (0, 4 * tile)
            for place in hole:
                tiles[layer, a * tile:(a + 1) * tile, place:place + tile] = jnp.zeros(
                    (tile, tile), jnp.bfloat16
                )

    for layer in outer:
        merge(layer)
    pl.semaphore_wait(barrier, len(greeted))

    sent = []

    def send(source, target, device):
        n = len(sent)
        copy = pltpu.make_async_remote_copy(
            src_ref=source, dst_ref=target, send_sem=send_sem.at[n], recv_sem=recv_sem.at[n],
            device_id=device, device_id_type=MESH,
        )
        copy.start()
        sent.append(copy)
        return copy

    tile_copies = {}

    def send_tiles(layer):
        tile_copies[layer] = []
        for a in range(FACE):
            for start, place, size in spans(a):
                tile_copies[layer].append(send(
                    pieces.at[layer * FACE + a, :, pl.ds(start, size)],
                    tiles.at[layer, pl.ds(pl.multiple_of(a * tile + mine, part), part), pl.ds(place, size)],
                    {"band": other},
                ))

    def send_halo(k, c, up):
        if up:
            return send(ext[k].at[c, pl.ds(rows, face)], ext[k].at[c, pl.ds(0, face)], {"slab": after})
        return send(
            ext[k].at[c, pl.ds(face, face)], ext[k].at[c, pl.ds(rows + face, face)], {"slab": before}
        )

    for layer in outer:
        send_tiles(layer)
    halos = {}
    for c in range(chunks):
        loads[c].wait()
        halos[0, c] = [send_halo(0, c, False), send_halo(0, c, True)]
    for layer in inner_layers:
        merge(layer)
        send_tiles(layer)

    def apply_layer(k, c, layer):
        product = jnp.dot(
            tiles[layer], ext[k][c, layer * face:(layer + 3) * face, :],
            preferred_element_type=jnp.float32,
        )
        inner = slice((layer + 1) * face, (layer + 2) * face)
        if k == 1 or k == 2:
            product = 2.0 * product - ext[k - 1][c, inner, :].astype(jnp.float32)
        if k < 3:
            ext[k + 1][c, inner, :] = product.astype(jnp.bfloat16)
        else:
            own_applied[c, layer * face:(layer + 1) * face, :] = product.astype(jnp.bfloat16)

    strip_copies = {}
    mine_at = pl.multiple_of(band * strip, strip)
    theirs_at = pl.multiple_of(other * strip, strip)

    def send_strip(which, c, source, base):
        place = strip3 if which == 3 else strip4
        group = band * chunks + c
        strip_copies[which, c] = send(
            source.at[c, pl.ds(base + theirs_at, strip)], place.at[group], {"band": other}
        )
        place[group] = source[c, pl.ds(base + mine_at, strip), :]

    def outer_layer(k, c, layer):
        halos[k, c][1 if layer == 0 else 0].wait_recv()
        apply_layer(k, c, layer)
        if k < 3:
            halos.setdefault((k + 1, c), []).append(send_halo(k + 1, c, layer != 0))

    for layer in outer:
        for copy in tile_copies[layer]:
            copy.wait_recv()
        for c in range(chunks):
            outer_layer(0, c, layer)
    for layer in inner_layers:
        for copy in tile_copies[layer]:
            copy.wait_recv()
        for c in range(chunks):
            apply_layer(0, c, layer)
    for k in range(1, 4):
        for c in range(chunks):
            for layer in inner_layers:
                apply_layer(k, c, layer)
        for c in range(chunks):
            for layer in outer:
                outer_layer(k, c, layer)
            if k == 2:
                send_strip(3, c, ext3, face)
            if k == 3:
                send_strip(4, c, own_applied, 0)

    def transposed_dot(left, right):
        return lax.dot_general(
            left, right, (((0,), (0,)), ((), ())), preferred_element_type=jnp.float32
        )

    def unit_start(unit, left, right):
        to_core[unit] = transposed_dot(left(1 - core), right).astype(jnp.bfloat16)
        copy = send(to_core.at[unit], from_core.at[unit], sibling)
        own32[unit] = transposed_dot(left(core), right)
        return copy

    def unit_spread(unit, copy, place, first, plane):
        copy.wait_recv()
        to_peers[unit] = (own32[unit] + from_core[unit].astype(jnp.float32)).astype(jnp.bfloat16)
        copies = []
        for j in range(first, chips):
            target = ring(j)
            copies.append(send(
                to_peers.at[unit, pl.ds(pl.multiple_of(target * piece, piece), piece)],
                from_peers.at[place + j],
                at_chip(target, plane),
            ))
        return copies

    my_piece = pl.multiple_of(chip * piece, piece)

    def summed(unit, places, quad, c):
        total = to_peers[unit, pl.ds(my_piece, piece), :].astype(jnp.float32)
        for place in places:
            total = total + from_peers[place].astype(jnp.float32)
        row = pl.multiple_of(core * width + my_piece, piece)
        gram16[quad * chunks + c, pl.ds(row, piece), :] = (total * gram_scale).astype(jnp.bfloat16)

    def pass_on(quad, index, device, span):
        row = pl.multiple_of(core * width + index * piece, piece)
        ref = gram16.at[pl.ds(quad * chunks + span[0], span[1]), pl.ds(row, piece)]
        return send(ref, ref, device)

    def place_of(c, kind):
        return (c * 3 + kind) * chips

    diag = [c for c in range(chunks)]
    near = [chunks + c for c in range(chunks)]
    cross = [2 * chunks + c for c in range(chunks)]

    starts = [
        unit_start(diag[c], lambda d: ext3[d, face:face + rows, :], own_applied[c])
        for c in range(chunks)
    ]
    diag_pieces = [
        unit_spread(diag[c], starts[c], place_of(c, 0), 1, band) for c in range(chunks)
    ]
    for c in range(chunks):
        strip_copies[3, c].wait_recv()
    starts = [
        unit_start(near[c], lambda d: strip3[other * chunks + d], strip4[band * chunks + c])
        for c in range(chunks)
    ]
    near_pieces = [
        unit_spread(near[c], starts[c], place_of(c, 1), 1, band) for c in range(chunks)
    ]

    def level_chip(offset):
        return lax.rem(level + offset, depth) * 2 + column

    beside = level * 2 + (1 - column)
    own_diag, other_diag = band * 3, other * 3
    own_off, other_off = other * 2 + band, band * 2 + other

    class Round:
        def __init__(self, mine, theirs, span):
            self.mine, self.theirs, self.span = mine, theirs, span
            self.level_copies, self.side_copies = [], []
            self.across = pass_on(mine, chip, at_chip(chip, other), span)
            self.spread(mine)

        def spread(self, quad):
            self.side_copies.append(pass_on(quad, chip, at_chip(beside, band), self.span))
            for j in range(1, depth):
                copy = pass_on(quad, chip, at_chip(level_chip(j), band), self.span)
                self.level_copies.append((quad, j, copy))

        def second(self):
            self.across.wait_recv()
            self.spread(self.theirs)

        def forward(self):
            for quad, j, copy in self.level_copies:
                copy.wait_recv()
                index = level_chip(depth - j)
                self.side_copies.append(pass_on(quad, index, at_chip(beside, band), self.span))

        def to_sibling(self):
            for copy in self.side_copies:
                copy.wait_recv()
            row = pl.multiple_of(core * width, width)
            copies = []
            for quad in (self.mine, self.theirs):
                ref = gram16.at[pl.ds(quad * chunks + self.span[0], self.span[1]), pl.ds(row, width)]
                copies.append(send(ref, ref, sibling))
            return copies

    def cross_unit(c):
        strip_copies[4, c].wait_recv()
        start = unit_start(cross[c], lambda d: strip3[band * chunks + d], strip4[other * chunks + c])
        return unit_spread(cross[c], start, place_of(c, 2), 0, other)

    def sum_off(c, cross_copies):
        for copy in near_pieces[c] + cross_copies:
            copy.wait_recv()
        places = [place_of(c, 1) + j for j in range(1, chips)]
        places += [place_of(c, 2) + j for j in range(chips)]
        summed(near[c], places, own_off, c)

    for c in range(chunks):
        for copy in diag_pieces[c]:
            copy.wait_recv()
        summed(diag[c], [place_of(c, 0) + j for j in range(1, chips)], own_diag, c)
    rounds = [Round(own_diag, other_diag, (0, chunks))]
    rounds[0].second()
    cross_copies = cross_unit(0)
    rounds[0].forward()
    last = chunks - 1
    for c in range(last):
        sum_off(c, cross_copies)
        rounds.append(Round(own_off, other_off, (c, 1)))
        cross_copies = cross_unit(c + 1)
        rounds[-1].second()
    early_copies = rounds[0].to_sibling()
    for turn in rounds[1:]:
        turn.forward()

    sum_off(last, cross_copies)
    span = (last, 1)
    plane_copies, core_copies = [], []

    def spread_plane(index):
        plane_copies.append((index, [
            pass_on(own_off, index, at_chip(chip, other), span),
            pass_on(own_off, index, at_chip(beside, band), span),
            pass_on(own_off, index, at_chip(beside, other), span),
        ]))
        core_copies.append(pass_on(own_off, index, sibling, span))

    level_copies = [
        (j, pass_on(own_off, chip, at_chip(level_chip(j), band), span)) for j in range(1, depth)
    ]
    spread_plane(chip)
    for j, copy in level_copies:
        copy.wait_recv()
        spread_plane(level_chip(depth - j))
    for turn in rounds[1:]:
        early_copies += turn.to_sibling()

    def mix(gr, gc, c):
        block = gram16[(gr * 2 + gc) * chunks + c]
        total = jnp.zeros((strip, width), jnp.float32)
        for d in range(chunks):
            total += jnp.dot(
                strip3[gr * chunks + d], block[d * width:(d + 1) * width],
                preferred_element_type=jnp.float32,
            )
        return total

    def finish(gc, c):
        q = gc * chunks + c
        out_ref[:, q * width:(q + 1) * width] = (out32[gc] - mix(1 - gc, gc, c)).astype(jnp.bfloat16)

    def begin(gc, c):
        out32[gc] = strip4[gc * chunks + c].astype(jnp.float32) - mix(gc, gc, c)

    for copy in early_copies:
        copy.wait_recv()
    for c in range(last):
        for gc in range(2):
            begin(gc, c)
            finish(gc, c)
    for gc in range(2):
        begin(gc, last)
    for index, (over, aside, corner) in plane_copies:
        apart = index + 1 - 2 * column
        over.wait_recv()
        core_copies.append(pass_on(other_off, index, sibling, span))
        aside.wait_recv()
        core_copies.append(pass_on(own_off, apart, sibling, span))
        corner.wait_recv()
        core_copies.append(pass_on(other_off, apart, sibling, span))
    for copy in core_copies:
        copy.wait_recv()
    for gc in range(2):
        finish(gc, last)
    assert len(sent) <= send_sem.shape[0]
    for copy in sent:
        copy.wait_send()


def fused_body(slabs, hamiltonian, neighbors, orbitals):
    blocks, slots, part, tile = hamiltonian.shape
    rows, bands = orbitals.shape
    layers = blocks // FACE
    width = bands // CHUNKS
    groups = 2 * CHUNKS
    strip = rows // 2
    face = FACE * tile
    chips, depth = slabs // 2, slabs // 4
    piece = width // chips
    units = 3 * CHUNKS
    gram_scale = 1.0 / math.sqrt(float(rows * slabs) * float(bands * 2))
    copies = 2 * blocks + 8 * CHUNKS + 2 * CHUNKS + units * (chips + 1) + 4 * depth + 5
    copies += (CHUNKS - 1) * (4 * depth + 3) + 8 * depth
    half = jnp.bfloat16
    flops = 2 * rows * 6 * tile * bands * 4 + 2 * 2 * strip * 4 * bands * bands
    return pl.pallas_call(
        functools.partial(kernel, slabs, gram_scale),
        out_shape=jax.ShapeDtypeStruct((strip, 2 * bands), half),
        in_specs=[
            pl.BlockSpec(memory_space=pltpu.SMEM),
            pl.BlockSpec(memory_space=pl.ANY),
            pl.BlockSpec(memory_space=pl.ANY),
        ],
        out_specs=pl.BlockSpec(memory_space=pltpu.VMEM),
        scratch_shapes=[
            pltpu.VMEM((blocks, slots, part, tile), half),
            pltpu.VMEM((blocks, part, 4 * tile), half),
            pltpu.VMEM((layers, face, 3 * face), half),
            *[pltpu.VMEM((CHUNKS, rows + 2 * face, width), half) for _ in range(4)],
            pltpu.VMEM((CHUNKS, rows, width), half),
            pltpu.VMEM((groups, strip, width), half),
            pltpu.VMEM((groups, strip, width), half),
            pltpu.VMEM((units, width, width), jnp.float32),
            pltpu.VMEM((units, width, width), half),
            pltpu.VMEM((units, width, width), half),
            pltpu.VMEM((units, width, width), half),
            pltpu.VMEM((units * chips, piece, width), half),
            pltpu.VMEM((4 * CHUNKS, CHUNKS * width, width), half),
            pltpu.VMEM((2, strip, width), jnp.float32),
            pltpu.SemaphoreType.DMA((CHUNKS + layers,)),
            pltpu.SemaphoreType.DMA((copies,)),
            pltpu.SemaphoreType.DMA((copies,)),
        ],
        compiler_params=pltpu.CompilerParams(
            collective_id=0, has_side_effects=True, vmem_limit_bytes=48 * 1024 * 1024
        ),
        cost_estimate=pl.CostEstimate(flops=flops, bytes_accessed=4 * rows * bands, transcendentals=0),
    )(neighbors, hamiltonian, orbitals)


def solution(mesh):
    in_specs = (P("slab", None, "band", None), P("slab", None), P("slab", "band"))
    out_specs = P(("slab", "band"), None)
    slabs, groups = mesh.shape["slab"], mesh.shape["band"]
    pairs = groups == 2 and slabs >= 8 and slabs % 4 == 0 and CHUNKS == 2
    body = functools.partial(fused_body, slabs) if pairs else plain_body
    return jax.shard_map(body, mesh=mesh, in_specs=in_specs, out_specs=out_specs, check_vma=False)
```

```python
import functools
import math

import jax
import jax.numpy as jnp
from jax import lax
from jax.experimental import pallas as pl
from jax.experimental.pallas import tpu as pltpu
from jax.sharding import PartitionSpec as P

FACE = 2
CHUNKS = 2
MESH = pl.DeviceIdType.MESH


def padded(block, sides, width):
    for axis, dim in sides:
        count = lax.axis_size(axis)
        forward = [(i, i + 1) for i in range(count - 1)]
        forward.append((count - 1, 0))
        backward = [(target, source) for source, target in forward]
        low = lax.ppermute(
            lax.slice_in_dim(block, block.shape[dim] - width, None, axis=dim), axis, forward
        )
        high = lax.ppermute(lax.slice_in_dim(block, 0, width, axis=dim), axis, backward)
        block = jnp.concatenate([low, block, high], axis=dim)
    return block


def apply_local(vector, full_tiles, neighbors):
    tile_size = full_tiles.shape[2]
    extended = padded(vector, (("slab", 0),), FACE * tile_size)
    blocks = extended.reshape(-1, tile_size, vector.shape[1])
    picked_blocks = blocks[neighbors]
    product = jnp.einsum(
        "rjab,rjbc->rac", full_tiles, picked_blocks, preferred_element_type=jnp.float32
    )
    return product.reshape(vector.shape[0], vector.shape[1])


def plain_body(hamiltonian, neighbors, orbitals):
    full_tiles = lax.all_gather(hamiltonian, "band", axis=2, tiled=True)
    first = apply_local(orbitals, full_tiles, neighbors).astype(jnp.bfloat16)
    second = (
        2.0 * apply_local(first, full_tiles, neighbors) - orbitals.astype(jnp.float32)
    ).astype(jnp.bfloat16)
    third = (2.0 * apply_local(second, full_tiles, neighbors) - first.astype(jnp.float32)).astype(
        jnp.bfloat16
    )
    applied = apply_local(third, full_tiles, neighbors).astype(jnp.bfloat16)
    rows_all = orbitals.shape[0] * lax.axis_size("slab")
    bands_all = orbitals.shape[1] * lax.axis_size("band")
    gram_scale = 1.0 / math.sqrt(float(rows_all) * float(bands_all))
    strip_third, strip_applied = (
        lax.all_to_all(third, "band", split_axis=0, concat_axis=1, tiled=True),
        lax.all_to_all(applied, "band", split_axis=0, concat_axis=1, tiled=True),
    )
    row_block = lax.psum_scatter(
        jnp.einsum(
            "rb,rc->bc", strip_third, strip_applied, preferred_element_type=jnp.float32
        ).astype(jnp.bfloat16),
        "band",
        scatter_dimension=0,
        tiled=True,
    ).astype(jnp.float32)
    slab_summed = lax.psum(row_block, "slab")
    gram_block = (slab_summed * gram_scale).astype(jnp.bfloat16)
    mixed = jnp.dot(
        strip_third,
        lax.all_gather(gram_block, "band", axis=0, tiled=True),
        preferred_element_type=jnp.float32,
    )
    return (strip_applied.astype(jnp.float32) - mixed).astype(jnp.bfloat16)


def kernel(
    slabs, gram_scale, neighbors_ref, hamiltonian_ref, orbitals_ref, out_ref,
    names, slots, pieces, tiles, ext0, ext1, ext2, ext3, own_applied, strip3, strip4, own32, to_core, from_core,
    to_peers, from_peers, crossing, gram16, out32, local_sem, send_sem, recv_sem,
):
    slab, band = lax.axis_index("slab"), lax.axis_index("band")
    other = 1 - band
    after, before = lax.rem(slab + 1, slabs), lax.rem(slab + slabs - 1, slabs)
    blocks, _, part, _ = slots.shape
    tile = 2 * part
    layers = blocks // FACE
    face = FACE * tile
    rows = blocks * tile
    chunks, _, width = ext0.shape
    strip = rows // 2
    groups = 2 * chunks
    ext = [ext0, ext1, ext2, ext3]

    chips, depth = slabs // 2, slabs // 4
    core, chip = lax.rem(slab, 2), lax.div(slab, 2)
    column, level = lax.rem(chip, 2), lax.div(chip, 2)
    sibling = {"slab": chip * 2 + (1 - core)}
    piece = width // chips

    def at_chip(index, plane):
        return {"slab": index * 2 + core, "band": plane}

    def ring(offset):
        return lax.rem(chip + offset, chips)

    barrier = pltpu.get_barrier_semaphore()
    greeted = [{"slab": after}, {"slab": before}, sibling]
    greeted += [at_chip(ring(j), band) for j in range(1, chips)]
    greeted += [at_chip(ring(j), other) for j in range(chips)]

    outer = [0, layers - 1]
    inner_layers = list(range(1, layers - 1))
    order = outer + inner_layers
    name_load = pltpu.make_async_copy(neighbors_ref, names, local_sem.at[chunks + layers])
    name_load.start()
    tile_loads = {}
    for layer in order:
        span = pl.ds(layer * FACE, FACE)
        tile_loads[layer] = pltpu.make_async_copy(
            hamiltonian_ref.at[span], slots.at[span], local_sem.at[chunks + layer]
        )
        tile_loads[layer].start()
    loads = []
    for c in range(chunks):
        load = pltpu.make_async_copy(
            orbitals_ref.at[:, pl.ds(c * width, width)],
            ext0.at[c, pl.ds(face, rows)],
            local_sem.at[c],
        )
        load.start()
        loads.append(load)
    for target in greeted:
        pl.semaphore_signal(barrier, inc=1, device_id=target, device_id_type=MESH)

    def spans(a):
        if a == 0:
            return ((0, 0, tile), (tile, 2 * tile, 3 * tile))
        return ((0, tile, 3 * tile), (3 * tile, 5 * tile, tile))

    mine = pl.multiple_of(band * part, part)

    def merge(layer):
        tile_loads[layer].wait()
        for a in range(FACE):
            row = layer * FACE + a
            sources = (row, FACE + layer * FACE, FACE + layer * FACE + 1, row + 2 * FACE)
            totals = [jnp.zeros((part, tile), jnp.float32) for _ in sources]
            for slot in range(slots.shape[1]):
                name = names[row, slot]
                entry = slots[row, slot].astype(jnp.float32)
                for n, source in enumerate(sources):
                    totals[n] = totals[n] + jnp.where(name == source, entry, 0.0)
            merged = jnp.concatenate([total.astype(jnp.bfloat16) for total in totals], axis=1)
            pieces[row] = merged
            for start, place, size in spans(a):
                tiles[layer, pl.ds(pl.multiple_of(a * tile + mine, part), part), place:place + size] = (
                    merged[:, start:start + size]
                )
            hole = (tile, 5 * tile) if a == 0 else (0, 4 * tile)
            for place in hole:
                tiles[layer, a * tile:(a + 1) * tile, place:place + tile] = jnp.zeros(
                    (tile, tile), jnp.bfloat16
                )

    name_load.wait()
    for layer in outer:
        merge(layer)
    pl.semaphore_wait(barrier, len(greeted))

    sent = []

    def send(source, target, device):
        n = len(sent)
        copy = pltpu.make_async_remote_copy(
            src_ref=source, dst_ref=target, send_sem=send_sem.at[n], recv_sem=recv_sem.at[n],
            device_id=device, device_id_type=MESH,
        )
        copy.start()
        sent.append(copy)
        return copy

    tile_copies = {}

    def send_tiles(layer):
        tile_copies[layer] = []
        for a in range(FACE):
            for start, place, size in spans(a):
                tile_copies[layer].append(send(
                    pieces.at[layer * FACE + a, :, pl.ds(start, size)],
                    tiles.at[layer, pl.ds(pl.multiple_of(a * tile + mine, part), part), pl.ds(place, size)],
                    {"band": other},
                ))

    def send_halo(k, c, up):
        if up:
            return send(ext[k].at[c, pl.ds(rows, face)], ext[k].at[c, pl.ds(0, face)], {"slab": after})
        return send(
            ext[k].at[c, pl.ds(face, face)], ext[k].at[c, pl.ds(rows + face, face)], {"slab": before}
        )

    for layer in outer:
        send_tiles(layer)
    halos = {}
    for c in range(chunks):
        loads[c].wait()
        halos[0, c] = [send_halo(0, c, False), send_halo(0, c, True)]
    for layer in inner_layers:
        merge(layer)
        send_tiles(layer)

    def apply_layer(k, c, layer):
        product = jnp.dot(
            tiles[layer], ext[k][c, layer * face:(layer + 3) * face, :],
            preferred_element_type=jnp.float32,
        )
        inner = slice((layer + 1) * face, (layer + 2) * face)
        if k == 1 or k == 2:
            product = 2.0 * product - ext[k - 1][c, inner, :].astype(jnp.float32)
        if k < 3:
            ext[k + 1][c, inner, :] = product.astype(jnp.bfloat16)
        else:
            own_applied[c, layer * face:(layer + 1) * face, :] = product.astype(jnp.bfloat16)

    strip_copies = {}
    mine_at = pl.multiple_of(band * strip, strip)
    theirs_at = pl.multiple_of(other * strip, strip)

    def send_strip(which, c, source, base):
        place = strip3 if which == 3 else strip4
        group = band * chunks + c
        strip_copies[which, c] = send(
            source.at[c, pl.ds(base + theirs_at, strip)], place.at[group], {"band": other}
        )

    def keep_strip(which, c, source, base):
        place = strip3 if which == 3 else strip4
        place[band * chunks + c] = source[c, pl.ds(base + mine_at, strip), :]

    def outer_layer(k, c, layer):
        halos[k, c][1 if layer == 0 else 0].wait_recv()
        apply_layer(k, c, layer)
        if k < 3:
            halos.setdefault((k + 1, c), []).append(send_halo(k + 1, c, layer != 0))

    for layer in outer:
        for copy in tile_copies[layer]:
            copy.wait_recv()
        for c in range(chunks):
            outer_layer(0, c, layer)
    for layer in inner_layers:
        for copy in tile_copies[layer]:
            copy.wait_recv()
        for c in range(chunks):
            apply_layer(0, c, layer)
    for k in range(1, 4):
        for c in range(chunks):
            for layer in inner_layers:
                apply_layer(k, c, layer)
        for c in range(chunks):
            for layer in outer:
                outer_layer(k, c, layer)
            if k == 2:
                send_strip(3, c, ext3, face)
                keep_strip(3, c, ext3, face)
            if k == 3:
                if c < chunks - 1:
                    send_strip(4, c, own_applied, 0)
                keep_strip(4, c, own_applied, 0)

    def transposed_dot(left, right):
        return lax.dot_general(
            left, right, (((0,), (0,)), ((), ())), preferred_element_type=jnp.float32
        )

    def unit_start(unit, left, right):
        to_core[unit] = transposed_dot(left(1 - core), right).astype(jnp.bfloat16)
        copy = send(to_core.at[unit], from_core.at[unit], sibling)
        own32[unit] = transposed_dot(left(core), right)
        return copy

    def unit_spread(unit, copy, place, first, plane):
        copy.wait_recv()
        to_peers[unit] = (own32[unit] + from_core[unit].astype(jnp.float32)).astype(jnp.bfloat16)
        copies = []
        for j in range(first, chips):
            target = ring(j)
            copies.append(send(
                to_peers.at[unit, pl.ds(pl.multiple_of(target * piece, piece), piece)],
                from_peers.at[place + j],
                at_chip(target, plane),
            ))
        return copies

    my_piece = pl.multiple_of(chip * piece, piece)

    def piece_sum(unit, places):
        total = to_peers[unit, pl.ds(my_piece, piece), :].astype(jnp.float32)
        for place in places:
            total = total + from_peers[place].astype(jnp.float32)
        return total

    def summed(unit, places, quad, c):
        total = piece_sum(unit, places)
        row = pl.multiple_of(core * width + my_piece, piece)
        gram16[quad * chunks + c, pl.ds(row, piece), :] = (total * gram_scale).astype(jnp.bfloat16)

    def pass_on(quad, index, device, span):
        row = pl.multiple_of(core * width + index * piece, piece)
        ref = gram16.at[pl.ds(quad * chunks + span[0], span[1]), pl.ds(row, piece)]
        return send(ref, ref, device)

    def place_of(c, kind):
        return (c * 3 + kind) * chips

    last = chunks - 1
    diag = [c for c in range(chunks)]
    near = [chunks + c for c in range(chunks)]
    cross = [2 * chunks + c for c in range(chunks)]

    starts = [
        unit_start(diag[c], lambda d: ext3[d, face:face + rows, :], own_applied[c])
        for c in range(chunks)
    ]
    diag_pieces = [
        unit_spread(diag[c], starts[c], place_of(c, 0), 1, band) for c in range(chunks)
    ]
    for c in range(chunks):
        strip_copies[3, c].wait_recv()
    starts = [
        unit_start(near[c], lambda d: strip3[other * chunks + d], strip4[band * chunks + c])
        for c in range(chunks)
    ]
    near_pieces = [
        unit_spread(near[c], starts[c], place_of(c, 1), 1, band) for c in range(chunks)
    ]

    def level_chip(offset):
        return lax.rem(level + offset, depth) * 2 + column

    beside = level * 2 + (1 - column)
    own_diag, other_diag = band * 3, other * 3
    own_off, other_off = other * 2 + band, band * 2 + other

    for c in range(chunks):
        for copy in diag_pieces[c]:
            copy.wait_recv()
        summed(diag[c], [place_of(c, 0) + j for j in range(1, chips)], own_diag, c)

    whole = (0, chunks)
    across = pass_on(own_diag, chip, at_chip(chip, other), whole)
    send_strip(4, last, own_applied, 0)
    diag_levels, diag_sides = [], []

    def spread_diag(quad):
        diag_sides.append(pass_on(quad, chip, at_chip(beside, band), whole))
        for j in range(1, depth):
            diag_levels.append((quad, j, pass_on(quad, chip, at_chip(level_chip(j), band), whole)))

    def block_to_sibling(quad, span):
        row = pl.multiple_of(core * width, width)
        ref = gram16.at[pl.ds(quad * chunks + span[0], span[1]), pl.ds(row, width)]
        return send(ref, ref, sibling)

    spread_diag(own_diag)

    def cross_unit(c, first, plane):
        strip_copies[4, c].wait_recv()
        start = unit_start(cross[c], lambda d: strip3[band * chunks + d], strip4[other * chunks + c])
        return unit_spread(cross[c], start, place_of(c, 2), first, plane)

    cross_copies = {c: cross_unit(c, 1, band) for c in range(last)}
    across.wait_recv()
    spread_diag(other_diag)
    for c in range(last):
        for copy in cross_copies[c]:
            copy.wait_recv()
        total = piece_sum(cross[c], [place_of(c, 2) + j for j in range(1, chips)])
        crossing[c] = total.astype(jnp.bfloat16)
        cross_copies[c] = [send(crossing.at[c], from_peers.at[place_of(c, 2)], at_chip(chip, other))]
    for quad, j, copy in diag_levels:
        copy.wait_recv()
        diag_sides.append(pass_on(quad, level_chip(depth - j), at_chip(beside, band), whole))
    cross_copies[last] = cross_unit(last, 0, other)
    for copy in diag_sides:
        copy.wait_recv()
    early_copies = [block_to_sibling(quad, whole) for quad in (own_diag, other_diag)]

    def sum_off(c):
        for copy in near_pieces[c] + cross_copies[c]:
            copy.wait_recv()
        places = [place_of(c, 1) + j for j in range(1, chips)]
        places += [place_of(c, 2) + j for j in range(chips if c == last else 1)]
        summed(near[c], places, own_off, c)

    def spread_plane(index, span):
        return [
            pass_on(own_off, index, at_chip(chip, other), span),
            pass_on(own_off, index, at_chip(beside, band), span),
            pass_on(own_off, index, at_chip(beside, other), span),
        ]

    plane_copies = {}
    for c in range(chunks):
        sum_off(c)
        span = (c, 1)
        level_copies = [
            (j, pass_on(own_off, chip, at_chip(level_chip(j), band), span))
            for j in range(1, depth)
        ]
        plane_copies[c] = spread_plane(chip, span)
        for j, copy in level_copies:
            copy.wait_recv()
            plane_copies[c] += spread_plane(level_chip(depth - j), span)

    def mix(gr, gc, c):
        block = gram16[(gr * 2 + gc) * chunks + c]
        total = jnp.zeros((strip, width), jnp.float32)
        for d in range(chunks):
            total += jnp.dot(
                strip3[gr * chunks + d], block[d * width:(d + 1) * width],
                preferred_element_type=jnp.float32,
            )
        return total

    for copy in early_copies:
        copy.wait_recv()
    for gc in range(2):
        for c in range(chunks):
            q = gc * chunks + c
            out32[q] = strip4[q].astype(jnp.float32) - mix(gc, gc, c)
    core_copies = {}
    for c in range(chunks):
        for copy in plane_copies[c]:
            copy.wait_recv()
        core_copies[c] = [block_to_sibling(quad, (c, 1)) for quad in (own_off, other_off)]
    for c in range(chunks):
        for copy in core_copies[c]:
            copy.wait_recv()
        for gc in range(2):
            q = gc * chunks + c
            out_ref[:, q * width:(q + 1) * width] = (out32[q] - mix(1 - gc, gc, c)).astype(
                jnp.bfloat16
            )
    assert len(sent) <= send_sem.shape[0]
    for copy in sent:
        copy.wait_send()


def fused_body(slabs, hamiltonian, neighbors, orbitals):
    blocks, slots, part, tile = hamiltonian.shape
    rows, bands = orbitals.shape
    layers = blocks // FACE
    width = bands // CHUNKS
    groups = 2 * CHUNKS
    strip = rows // 2
    face = FACE * tile
    chips, depth = slabs // 2, slabs // 4
    piece = width // chips
    units = 3 * CHUNKS
    gram_scale = 1.0 / math.sqrt(float(rows * slabs) * float(bands * 2))
    copies = 2 * blocks + 8 * CHUNKS + 2 * CHUNKS + units * (chips + 1) + 4 * depth + 5
    copies += CHUNKS * (4 * depth + 4)
    half = jnp.bfloat16
    flops = 2 * rows * 6 * tile * bands * 4 + 2 * 2 * strip * 4 * bands * bands
    return pl.pallas_call(
        functools.partial(kernel, slabs, gram_scale),
        out_shape=jax.ShapeDtypeStruct((strip, 2 * bands), half),
        in_specs=[
            pl.BlockSpec(memory_space=pltpu.HBM),
            pl.BlockSpec(memory_space=pltpu.HBM),
            pl.BlockSpec(memory_space=pltpu.HBM),
        ],
        out_specs=pl.BlockSpec(memory_space=pltpu.VMEM),
        scratch_shapes=[
            pltpu.SMEM((blocks, slots), jnp.int32),
            pltpu.VMEM((blocks, slots, part, tile), half),
            pltpu.VMEM((blocks, part, 4 * tile), half),
            pltpu.VMEM((layers, face, 3 * face), half),
            *[pltpu.VMEM((CHUNKS, rows + 2 * face, width), half) for _ in range(4)],
            pltpu.VMEM((CHUNKS, rows, width), half),
            pltpu.VMEM((groups, strip, width), half),
            pltpu.VMEM((groups, strip, width), half),
            pltpu.VMEM((units, width, width), jnp.float32),
            pltpu.VMEM((units, width, width), half),
            pltpu.VMEM((units, width, width), half),
            pltpu.VMEM((units, width, width), half),
            pltpu.VMEM((units * chips, piece, width), half),
            pltpu.VMEM((CHUNKS, piece, width), half),
            pltpu.VMEM((4 * CHUNKS, CHUNKS * width, width), half),
            pltpu.VMEM((groups, strip, width), jnp.float32),
            pltpu.SemaphoreType.DMA((CHUNKS + layers + 1,)),
            pltpu.SemaphoreType.DMA((copies,)),
            pltpu.SemaphoreType.DMA((copies,)),
        ],
        compiler_params=pltpu.CompilerParams(
            collective_id=0, has_side_effects=True, vmem_limit_bytes=63 * 1024 * 1024 + 512 * 1024
        ),
        cost_estimate=pl.CostEstimate(flops=flops, bytes_accessed=4 * rows * bands, transcendentals=0),
    )(neighbors, hamiltonian, orbitals)


def solution(mesh):
    in_specs = (P("slab", None, "band", None), P("slab", None), P("slab", "band"))
    out_specs = P(("slab", "band"), None)
    slabs, groups = mesh.shape["slab"], mesh.shape["band"]
    pairs = groups == 2 and slabs >= 8 and slabs % 4 == 0 and CHUNKS == 2
    body = functools.partial(fused_body, slabs) if pairs else plain_body
    return jax.shard_map(body, mesh=mesh, in_specs=in_specs, out_specs=out_specs, check_vma=False)
```

```python
import functools
import math

import jax
import jax.numpy as jnp
from jax import lax
from jax.experimental import pallas as pl
from jax.experimental.pallas import tpu as pltpu
from jax.sharding import PartitionSpec as P

FACE = 2
CHUNKS = 2
MESH = pl.DeviceIdType.MESH


def padded(block, sides, width):
    for axis, dim in sides:
        count = lax.axis_size(axis)
        forward = [(i, i + 1) for i in range(count - 1)]
        forward.append((count - 1, 0))
        backward = [(target, source) for source, target in forward]
        low = lax.ppermute(
            lax.slice_in_dim(block, block.shape[dim] - width, None, axis=dim), axis, forward
        )
        high = lax.ppermute(lax.slice_in_dim(block, 0, width, axis=dim), axis, backward)
        block = jnp.concatenate([low, block, high], axis=dim)
    return block


def apply_local(vector, full_tiles, neighbors):
    tile_size = full_tiles.shape[2]
    extended = padded(vector, (("slab", 0),), FACE * tile_size)
    blocks = extended.reshape(-1, tile_size, vector.shape[1])
    picked_blocks = blocks[neighbors]
    product = jnp.einsum(
        "rjab,rjbc->rac", full_tiles, picked_blocks, preferred_element_type=jnp.float32
    )
    return product.reshape(vector.shape[0], vector.shape[1])


def plain_body(hamiltonian, neighbors, orbitals):
    full_tiles = lax.all_gather(hamiltonian, "band", axis=2, tiled=True)
    first = apply_local(orbitals, full_tiles, neighbors).astype(jnp.bfloat16)
    second = (
        2.0 * apply_local(first, full_tiles, neighbors) - orbitals.astype(jnp.float32)
    ).astype(jnp.bfloat16)
    third = (2.0 * apply_local(second, full_tiles, neighbors) - first.astype(jnp.float32)).astype(
        jnp.bfloat16
    )
    applied = apply_local(third, full_tiles, neighbors).astype(jnp.bfloat16)
    rows_all = orbitals.shape[0] * lax.axis_size("slab")
    bands_all = orbitals.shape[1] * lax.axis_size("band")
    gram_scale = 1.0 / math.sqrt(float(rows_all) * float(bands_all))
    strip_third, strip_applied = (
        lax.all_to_all(third, "band", split_axis=0, concat_axis=1, tiled=True),
        lax.all_to_all(applied, "band", split_axis=0, concat_axis=1, tiled=True),
    )
    row_block = lax.psum_scatter(
        jnp.einsum(
            "rb,rc->bc", strip_third, strip_applied, preferred_element_type=jnp.float32
        ).astype(jnp.bfloat16),
        "band",
        scatter_dimension=0,
        tiled=True,
    ).astype(jnp.float32)
    slab_summed = lax.psum(row_block, "slab")
    gram_block = (slab_summed * gram_scale).astype(jnp.bfloat16)
    mixed = jnp.dot(
        strip_third,
        lax.all_gather(gram_block, "band", axis=0, tiled=True),
        preferred_element_type=jnp.float32,
    )
    return (strip_applied.astype(jnp.float32) - mixed).astype(jnp.bfloat16)


def kernel(
    slabs, gram_scale, neighbors_ref, hamiltonian_ref, orbitals_ref, out_ref,
    names, slots, pieces, arrived, tiles, slab_t, other_t, ext0, ext1, ext2, ext3, own_applied, strip3, strip4, own32, to_core, from_core,
    to_peers, from_peers, crossing, gram16, out32, local_sem, send_sem, recv_sem,
):
    slab, band = lax.axis_index("slab"), lax.axis_index("band")
    other = 1 - band
    after, before = lax.rem(slab + 1, slabs), lax.rem(slab + slabs - 1, slabs)
    blocks, _, part, _ = slots.shape
    tile = 2 * part
    layers = blocks // FACE
    face = FACE * tile
    rows = blocks * tile
    chunks, _, width = ext0.shape
    strip = rows // 2
    groups = 2 * chunks
    ext = [ext0, ext1, ext2, ext3]

    chips, depth = slabs // 2, slabs // 4
    core, chip = lax.rem(slab, 2), lax.div(slab, 2)
    column, level = lax.rem(chip, 2), lax.div(chip, 2)
    sibling = {"slab": chip * 2 + (1 - core)}
    piece = width // chips

    def at_chip(index, plane):
        return {"slab": index * 2 + core, "band": plane}

    def ring(offset):
        return lax.rem(chip + offset, chips)

    barrier = pltpu.get_barrier_semaphore()
    greeted = [{"slab": after}, {"slab": before}, sibling]
    greeted += [at_chip(ring(j), band) for j in range(1, chips)]
    greeted += [at_chip(ring(j), other) for j in range(chips)]

    outer = [0, layers - 1]
    inner_layers = list(range(1, layers - 1))
    order = outer + inner_layers
    name_load = pltpu.make_async_copy(neighbors_ref, names, local_sem.at[chunks + layers])
    name_load.start()
    tile_loads = {}
    for layer in order:
        span = pl.ds(layer * FACE, FACE)
        tile_loads[layer] = pltpu.make_async_copy(
            hamiltonian_ref.at[span], slots.at[span], local_sem.at[chunks + layer]
        )
        tile_loads[layer].start()
    loads = []
    for c in range(chunks):
        load = pltpu.make_async_copy(
            orbitals_ref.at[:, pl.ds(c * width, width)],
            ext0.at[c, pl.ds(face, rows)],
            local_sem.at[c],
        )
        load.start()
        loads.append(load)
    for target in greeted:
        pl.semaphore_signal(barrier, inc=1, device_id=target, device_id_type=MESH)

    def spans(a):
        if a == 0:
            return ((0, 0, tile), (tile, 2 * tile, 3 * tile))
        return ((0, tile, 3 * tile), (3 * tile, 5 * tile, tile))

    def put(layer, a, side, merged):
        row = pl.multiple_of(a * tile + side * part, part)
        for start, place, size in spans(a):
            tiles[layer, pl.ds(row, part), place:place + size] = merged[:, start:start + size]

    def merge(layer):
        tile_loads[layer].wait()
        for a in range(FACE):
            row = layer * FACE + a
            sources = (row, FACE + layer * FACE, FACE + layer * FACE + 1, row + 2 * FACE)
            totals = [jnp.zeros((part, tile), jnp.float32) for _ in sources]
            for slot in range(slots.shape[1]):
                name = names[row, slot]
                entry = slots[row, slot].astype(jnp.float32)
                for n, source in enumerate(sources):
                    totals[n] = totals[n] + jnp.where(name == source, entry, 0.0)
            merged = jnp.concatenate([total.astype(jnp.bfloat16) for total in totals], axis=1)
            pieces[layer, a] = merged
            put(layer, a, band, merged)
            hole = (tile, 5 * tile) if a == 0 else (0, 4 * tile)
            for place in hole:
                tiles[layer, a * tile:(a + 1) * tile, place:place + tile] = jnp.zeros(
                    (tile, tile), jnp.bfloat16
                )

    name_load.wait()
    for layer in outer:
        merge(layer)
    pl.semaphore_wait(barrier, len(greeted))

    sent = []

    def send(source, target, device):
        n = len(sent)
        copy = pltpu.make_async_remote_copy(
            src_ref=source, dst_ref=target, send_sem=send_sem.at[n], recv_sem=recv_sem.at[n],
            device_id=device, device_id_type=MESH,
        )
        copy.start()
        sent.append(copy)
        return copy

    tile_copies = {}

    def send_tiles(layer):
        tile_copies[layer] = send(pieces.at[layer], arrived.at[layer], {"band": other})

    def place_tiles(layer):
        tile_copies[layer].wait_recv()
        for a in range(FACE):
            put(layer, a, other, arrived[layer, a])

    def send_halo(k, c, up):
        if up:
            return send(ext[k].at[c, pl.ds(rows, face)], ext[k].at[c, pl.ds(0, face)], {"slab": after})
        return send(
            ext[k].at[c, pl.ds(face, face)], ext[k].at[c, pl.ds(rows + face, face)], {"slab": before}
        )

    for layer in outer:
        send_tiles(layer)
    halos = {}
    for c in range(chunks):
        loads[c].wait()
        halos[0, c] = [send_halo(0, c, False), send_halo(0, c, True)]
    for layer in inner_layers:
        merge(layer)
        send_tiles(layer)

    def apply_layer(k, c, layer):
        product = jnp.dot(
            tiles[layer], ext[k][c, layer * face:(layer + 3) * face, :],
            preferred_element_type=jnp.float32,
        )
        inner = slice((layer + 1) * face, (layer + 2) * face)
        if k == 1 or k == 2:
            product = 2.0 * product - ext[k - 1][c, inner, :].astype(jnp.float32)
        if k < 3:
            ext[k + 1][c, inner, :] = product.astype(jnp.bfloat16)
        else:
            own_applied[c, layer * face:(layer + 1) * face, :] = product.astype(jnp.bfloat16)

    strip_copies = {}
    mine_at = pl.multiple_of(band * strip, strip)
    theirs_at = pl.multiple_of(other * strip, strip)

    def send_strip(which, c, source, base):
        place = strip3 if which == 3 else strip4
        group = band * chunks + c
        strip_copies[which, c] = send(
            source.at[c, pl.ds(base + theirs_at, strip)], place.at[group], {"band": other}
        )

    def keep_strip(which, c, source, base):
        place = strip3 if which == 3 else strip4
        place[band * chunks + c] = source[c, pl.ds(base + mine_at, strip), :]

    def outer_layer(k, c, layer):
        halos[k, c][1 if layer == 0 else 0].wait_recv()
        apply_layer(k, c, layer)
        if k < 3:
            halos.setdefault((k + 1, c), []).append(send_halo(k + 1, c, layer != 0))

    for layer in outer:
        place_tiles(layer)
        for c in range(chunks):
            outer_layer(0, c, layer)
    for layer in inner_layers:
        place_tiles(layer)
        for c in range(chunks):
            apply_layer(0, c, layer)
    for k in range(1, 4):
        for c in range(chunks):
            for layer in inner_layers:
                apply_layer(k, c, layer)
        if k == 3:
            for c in range(chunks):
                slab_t[c] = ext3[c, face:face + rows, :].T
        for c in range(chunks):
            for layer in outer:
                outer_layer(k, c, layer)
            if k == 2:
                send_strip(3, c, ext3, face)
                keep_strip(3, c, ext3, face)
            if k == 3:
                if c < chunks - 1:
                    send_strip(4, c, own_applied, 0)
                keep_strip(4, c, own_applied, 0)

    def unit_start(unit, left, right):
        to_core[unit] = jnp.dot(
            left(1 - core), right, preferred_element_type=jnp.float32
        ).astype(jnp.bfloat16)
        copy = send(to_core.at[unit], from_core.at[unit], sibling)
        own32[unit] = jnp.dot(left(core), right, preferred_element_type=jnp.float32)
        return copy

    def unit_spread(unit, copy, place, first, plane):
        copy.wait_recv()
        to_peers[unit] = (own32[unit] + from_core[unit].astype(jnp.float32)).astype(jnp.bfloat16)
        copies = []
        for j in range(first, chips):
            target = ring(j)
            copies.append(send(
                to_peers.at[unit, pl.ds(pl.multiple_of(target * piece, piece), piece)],
                from_peers.at[place + j],
                at_chip(target, plane),
            ))
        return copies

    my_piece = pl.multiple_of(chip * piece, piece)

    def piece_sum(unit, places):
        total = to_peers[unit, pl.ds(my_piece, piece), :].astype(jnp.float32)
        for place in places:
            total = total + from_peers[place].astype(jnp.float32)
        return total

    def summed(unit, places, quad, c):
        total = piece_sum(unit, places)
        row = pl.multiple_of(core * width + my_piece, piece)
        gram16[quad * chunks + c, pl.ds(row, piece), :] = (total * gram_scale).astype(jnp.bfloat16)

    def pass_on(quad, index, device, span):
        row = pl.multiple_of(core * width + index * piece, piece)
        ref = gram16.at[pl.ds(quad * chunks + span[0], span[1]), pl.ds(row, piece)]
        return send(ref, ref, device)

    def place_of(c, kind):
        return (c * 3 + kind) * chips

    last = chunks - 1
    diag = [c for c in range(chunks)]
    near = [chunks + c for c in range(chunks)]
    cross = [2 * chunks + c for c in range(chunks)]

    starts = [
        unit_start(diag[c], lambda d: slab_t[d], own_applied[c])
        for c in range(chunks)
    ]
    diag_pieces = [
        unit_spread(diag[c], starts[c], place_of(c, 0), 1, band) for c in range(chunks)
    ]
    for c in range(chunks):
        strip_copies[3, c].wait_recv()
        other_t[c] = strip3[other * chunks + c].T
    starts = [
        unit_start(near[c], lambda d: other_t[d], strip4[band * chunks + c])
        for c in range(chunks)
    ]
    near_pieces = [
        unit_spread(near[c], starts[c], place_of(c, 1), 1, band) for c in range(chunks)
    ]

    def level_chip(offset):
        return lax.rem(level + offset, depth) * 2 + column

    beside = level * 2 + (1 - column)
    own_diag, other_diag = band * 3, other * 3
    own_off, other_off = other * 2 + band, band * 2 + other

    for c in range(chunks):
        for copy in diag_pieces[c]:
            copy.wait_recv()
        summed(diag[c], [place_of(c, 0) + j for j in range(1, chips)], own_diag, c)

    whole = (0, chunks)
    across = pass_on(own_diag, chip, at_chip(chip, other), whole)
    send_strip(4, last, own_applied, 0)
    diag_levels, diag_sides = [], []

    def spread_diag(quad):
        diag_sides.append(pass_on(quad, chip, at_chip(beside, band), whole))
        for j in range(1, depth):
            diag_levels.append((quad, j, pass_on(quad, chip, at_chip(level_chip(j), band), whole)))

    def block_to_sibling(quad, span):
        row = pl.multiple_of(core * width, width)
        ref = gram16.at[pl.ds(quad * chunks + span[0], span[1]), pl.ds(row, width)]
        return send(ref, ref, sibling)

    spread_diag(own_diag)

    def cross_unit(c, first, plane):
        strip_copies[4, c].wait_recv()
        start = unit_start(
            cross[c], lambda d: slab_t[d, :, pl.ds(mine_at, strip)], strip4[other * chunks + c]
        )
        return unit_spread(cross[c], start, place_of(c, 2), first, plane)

    cross_copies = {c: cross_unit(c, 1, band) for c in range(last)}
    across.wait_recv()
    spread_diag(other_diag)
    for c in range(last):
        for copy in cross_copies[c]:
            copy.wait_recv()
        total = piece_sum(cross[c], [place_of(c, 2) + j for j in range(1, chips)])
        crossing[c] = total.astype(jnp.bfloat16)
        cross_copies[c] = [send(crossing.at[c], from_peers.at[place_of(c, 2)], at_chip(chip, other))]
    for quad, j, copy in diag_levels:
        copy.wait_recv()
        diag_sides.append(pass_on(quad, level_chip(depth - j), at_chip(beside, band), whole))
    cross_copies[last] = cross_unit(last, 0, other)
    for copy in diag_sides:
        copy.wait_recv()
    early_copies = [block_to_sibling(quad, whole) for quad in (own_diag, other_diag)]

    def sum_off(c):
        for copy in near_pieces[c] + cross_copies[c]:
            copy.wait_recv()
        places = [place_of(c, 1) + j for j in range(1, chips)]
        places += [place_of(c, 2) + j for j in range(chips if c == last else 1)]
        summed(near[c], places, own_off, c)

    def spread_plane(index, span):
        return [
            pass_on(own_off, index, at_chip(chip, other), span),
            pass_on(own_off, index, at_chip(beside, band), span),
            pass_on(own_off, index, at_chip(beside, other), span),
        ]

    plane_copies = {}
    for c in range(chunks):
        sum_off(c)
        span = (c, 1)
        level_copies = [
            (j, pass_on(own_off, chip, at_chip(level_chip(j), band), span))
            for j in range(1, depth)
        ]
        plane_copies[c] = spread_plane(chip, span)
        for j, copy in level_copies:
            copy.wait_recv()
            plane_copies[c] += spread_plane(level_chip(depth - j), span)

    def mix(gr, gc, c):
        block = gram16[(gr * 2 + gc) * chunks + c]
        total = jnp.zeros((strip, width), jnp.float32)
        for d in range(chunks):
            total += jnp.dot(
                strip3[gr * chunks + d], block[d * width:(d + 1) * width],
                preferred_element_type=jnp.float32,
            )
        return total

    for copy in early_copies:
        copy.wait_recv()
    for gc in range(2):
        for c in range(chunks):
            q = gc * chunks + c
            out32[q] = strip4[q].astype(jnp.float32) - mix(gc, gc, c)
    core_copies = {}
    for c in range(chunks):
        for copy in plane_copies[c]:
            copy.wait_recv()
        core_copies[c] = [block_to_sibling(quad, (c, 1)) for quad in (own_off, other_off)]
    for c in range(chunks):
        for copy in core_copies[c]:
            copy.wait_recv()
        for gc in range(2):
            q = gc * chunks + c
            out_ref[:, q * width:(q + 1) * width] = (out32[q] - mix(1 - gc, gc, c)).astype(
                jnp.bfloat16
            )
    assert len(sent) <= send_sem.shape[0]
    for copy in sent:
        copy.wait_send()


def fused_body(slabs, hamiltonian, neighbors, orbitals):
    blocks, slots, part, tile = hamiltonian.shape
    rows, bands = orbitals.shape
    layers = blocks // FACE
    width = bands // CHUNKS
    groups = 2 * CHUNKS
    strip = rows // 2
    face = FACE * tile
    chips, depth = slabs // 2, slabs // 4
    piece = width // chips
    units = 3 * CHUNKS
    gram_scale = 1.0 / math.sqrt(float(rows * slabs) * float(bands * 2))
    copies = layers + 8 * CHUNKS + 2 * CHUNKS + units * (chips + 1) + 4 * depth + 5
    copies += CHUNKS * (4 * depth + 4)
    half = jnp.bfloat16
    flops = 2 * rows * 6 * tile * bands * 4 + 2 * 2 * strip * 4 * bands * bands
    return pl.pallas_call(
        functools.partial(kernel, slabs, gram_scale),
        out_shape=jax.ShapeDtypeStruct((strip, 2 * bands), half),
        in_specs=[
            pl.BlockSpec(memory_space=pltpu.HBM),
            pl.BlockSpec(memory_space=pltpu.HBM),
            pl.BlockSpec(memory_space=pltpu.HBM),
        ],
        out_specs=pl.BlockSpec(memory_space=pltpu.VMEM),
        scratch_shapes=[
            pltpu.SMEM((blocks, slots), jnp.int32),
            pltpu.VMEM((blocks, slots, part, tile), half),
            pltpu.VMEM((layers, FACE, part, 4 * tile), half),
            pltpu.VMEM((layers, FACE, part, 4 * tile), half),
            pltpu.VMEM((layers, face, 3 * face), half),
            pltpu.VMEM((CHUNKS, width, rows), half),
            pltpu.VMEM((CHUNKS, width, strip), half),
            *[pltpu.VMEM((CHUNKS, rows + 2 * face, width), half) for _ in range(4)],
            pltpu.VMEM((CHUNKS, rows, width), half),
            pltpu.VMEM((groups, strip, width), half),
            pltpu.VMEM((groups, strip, width), half),
            pltpu.VMEM((units, width, width), jnp.float32),
            pltpu.VMEM((units, width, width), half),
            pltpu.VMEM((units, width, width), half),
            pltpu.VMEM((units, width, width), half),
            pltpu.VMEM((units * chips, piece, width), half),
            pltpu.VMEM((CHUNKS, piece, width), half),
            pltpu.VMEM((4 * CHUNKS, CHUNKS * width, width), half),
            pltpu.VMEM((groups, strip, width), jnp.float32),
            pltpu.SemaphoreType.DMA((CHUNKS + layers + 1,)),
            pltpu.SemaphoreType.DMA((copies,)),
            pltpu.SemaphoreType.DMA((copies,)),
        ],
        compiler_params=pltpu.CompilerParams(
            collective_id=0, has_side_effects=True, vmem_limit_bytes=62 * 1024 * 1024 + 768 * 1024
        ),
        cost_estimate=pl.CostEstimate(flops=flops, bytes_accessed=4 * rows * bands, transcendentals=0),
    )(neighbors, hamiltonian, orbitals)


def solution(mesh):
    in_specs = (P("slab", None, "band", None), P("slab", None), P("slab", "band"))
    out_specs = P(("slab", "band"), None)
    slabs, groups = mesh.shape["slab"], mesh.shape["band"]
    pairs = groups == 2 and slabs >= 8 and slabs % 4 == 0 and CHUNKS == 2
    body = functools.partial(fused_body, slabs) if pairs else plain_body
    return jax.shard_map(body, mesh=mesh, in_specs=in_specs, out_specs=out_specs, check_vma=False)
```

```python
import functools
import math

import jax
import jax.numpy as jnp
from jax import lax
from jax.experimental import pallas as pl
from jax.experimental.pallas import tpu as pltpu
from jax.sharding import PartitionSpec as P

FACE = 2
CHUNKS = 2
MESH = pl.DeviceIdType.MESH


def padded(block, sides, width):
    for axis, dim in sides:
        count = lax.axis_size(axis)
        forward = [(i, i + 1) for i in range(count - 1)]
        forward.append((count - 1, 0))
        backward = [(target, source) for source, target in forward]
        low = lax.ppermute(
            lax.slice_in_dim(block, block.shape[dim] - width, None, axis=dim), axis, forward
        )
        high = lax.ppermute(lax.slice_in_dim(block, 0, width, axis=dim), axis, backward)
        block = jnp.concatenate([low, block, high], axis=dim)
    return block


def apply_local(vector, full_tiles, neighbors):
    tile_size = full_tiles.shape[2]
    extended = padded(vector, (("slab", 0),), FACE * tile_size)
    blocks = extended.reshape(-1, tile_size, vector.shape[1])
    picked_blocks = blocks[neighbors]
    product = jnp.einsum(
        "rjab,rjbc->rac", full_tiles, picked_blocks, preferred_element_type=jnp.float32
    )
    return product.reshape(vector.shape[0], vector.shape[1])


def plain_body(hamiltonian, neighbors, orbitals):
    full_tiles = lax.all_gather(hamiltonian, "band", axis=2, tiled=True)
    first = apply_local(orbitals, full_tiles, neighbors).astype(jnp.bfloat16)
    second = (
        2.0 * apply_local(first, full_tiles, neighbors) - orbitals.astype(jnp.float32)
    ).astype(jnp.bfloat16)
    third = (2.0 * apply_local(second, full_tiles, neighbors) - first.astype(jnp.float32)).astype(
        jnp.bfloat16
    )
    applied = apply_local(third, full_tiles, neighbors).astype(jnp.bfloat16)
    rows_all = orbitals.shape[0] * lax.axis_size("slab")
    bands_all = orbitals.shape[1] * lax.axis_size("band")
    gram_scale = 1.0 / math.sqrt(float(rows_all) * float(bands_all))
    strip_third, strip_applied = (
        lax.all_to_all(third, "band", split_axis=0, concat_axis=1, tiled=True),
        lax.all_to_all(applied, "band", split_axis=0, concat_axis=1, tiled=True),
    )
    row_block = lax.psum_scatter(
        jnp.einsum(
            "rb,rc->bc", strip_third, strip_applied, preferred_element_type=jnp.float32
        ).astype(jnp.bfloat16),
        "band",
        scatter_dimension=0,
        tiled=True,
    ).astype(jnp.float32)
    slab_summed = lax.psum(row_block, "slab")
    gram_block = (slab_summed * gram_scale).astype(jnp.bfloat16)
    mixed = jnp.dot(
        strip_third,
        lax.all_gather(gram_block, "band", axis=0, tiled=True),
        preferred_element_type=jnp.float32,
    )
    return (strip_applied.astype(jnp.float32) - mixed).astype(jnp.bfloat16)


def kernel(
    slabs, gram_scale, neighbors_ref, hamiltonian_ref, orbitals_ref, out_ref,
    names, slots, pieces, arrived, tiles, slab_t, other_t, ext0, ext1, ext2, ext3, own_applied, strip3, strip4, own32, to_core, from_core,
    to_peers, from_peers, crossing, gram16, out32, local_sem, send_sem, recv_sem,
):
    slab, band = lax.axis_index("slab"), lax.axis_index("band")
    other = 1 - band
    after, before = lax.rem(slab + 1, slabs), lax.rem(slab + slabs - 1, slabs)
    blocks, _, part, _ = slots.shape
    tile = 2 * part
    layers = blocks // FACE
    face = FACE * tile
    rows = blocks * tile
    chunks, _, width = ext0.shape
    strip = rows // 2
    groups = 2 * chunks
    ext = [ext0, ext1, ext2, ext3]

    chips, depth = slabs // 2, slabs // 4
    core, chip = lax.rem(slab, 2), lax.div(slab, 2)
    column, level = lax.rem(chip, 2), lax.div(chip, 2)
    sibling = {"slab": chip * 2 + (1 - core)}
    piece = width // chips

    def at_chip(index, plane):
        return {"slab": index * 2 + core, "band": plane}

    def ring(offset):
        return lax.rem(chip + offset, chips)

    barrier = pltpu.get_barrier_semaphore()
    greeted = [{"slab": after}, {"slab": before}, sibling]
    greeted += [at_chip(ring(j), band) for j in range(1, chips)]
    greeted += [at_chip(ring(j), other) for j in range(chips)]

    outer = [0, layers - 1]
    inner_layers = list(range(1, layers - 1))
    order = outer + inner_layers
    name_load = pltpu.make_async_copy(neighbors_ref, names, local_sem.at[chunks + layers])
    name_load.start()
    tile_loads = {}
    for layer in order:
        span = pl.ds(layer * FACE, FACE)
        tile_loads[layer] = pltpu.make_async_copy(
            hamiltonian_ref.at[span], slots.at[span], local_sem.at[chunks + layer]
        )
        tile_loads[layer].start()
    loads = []
    for c in range(chunks):
        load = pltpu.make_async_copy(
            orbitals_ref.at[:, pl.ds(c * width, width)],
            ext0.at[c, pl.ds(face, rows)],
            local_sem.at[c],
        )
        load.start()
        loads.append(load)
    for target in greeted:
        pl.semaphore_signal(barrier, inc=1, device_id=target, device_id_type=MESH)

    def spans(a):
        if a == 0:
            return ((0, 0, tile), (tile, 2 * tile, 3 * tile))
        return ((0, tile, 3 * tile), (3 * tile, 5 * tile, tile))

    def put(layer, a, side, merged):
        row = pl.multiple_of(a * tile + side * part, part)
        for start, place, size in spans(a):
            tiles[layer, pl.ds(row, part), place:place + size] = merged[:, start:start + size]

    def merge(layer):
        tile_loads[layer].wait()
        for a in range(FACE):
            row = layer * FACE + a
            sources = (row, FACE + layer * FACE, FACE + layer * FACE + 1, row + 2 * FACE)
            totals = [jnp.zeros((part, tile), jnp.float32) for _ in sources]
            for slot in range(slots.shape[1]):
                name = names[row, slot]
                entry = slots[row, slot].astype(jnp.float32)
                for n, source in enumerate(sources):
                    totals[n] = totals[n] + jnp.where(name == source, entry, 0.0)
            merged = jnp.concatenate([total.astype(jnp.bfloat16) for total in totals], axis=1)
            pieces[layer, a] = merged
            put(layer, a, band, merged)
            hole = (tile, 5 * tile) if a == 0 else (0, 4 * tile)
            for place in hole:
                tiles[layer, a * tile:(a + 1) * tile, place:place + tile] = jnp.zeros(
                    (tile, tile), jnp.bfloat16
                )

    name_load.wait()
    for layer in outer:
        merge(layer)
    pl.semaphore_wait(barrier, len(greeted))

    sent = []

    def send(source, target, device):
        n = len(sent)
        copy = pltpu.make_async_remote_copy(
            src_ref=source, dst_ref=target, send_sem=send_sem.at[n], recv_sem=recv_sem.at[n],
            device_id=device, device_id_type=MESH,
        )
        copy.start()
        sent.append(copy)
        return copy

    tile_copies = {}

    def send_tiles(layer):
        tile_copies[layer] = send(pieces.at[layer], arrived.at[layer], {"band": other})

    def place_tiles(layer):
        tile_copies[layer].wait_recv()
        for a in range(FACE):
            put(layer, a, other, arrived[layer, a])

    def send_halo(k, c, up):
        if up:
            return send(ext[k].at[c, pl.ds(rows, face)], ext[k].at[c, pl.ds(0, face)], {"slab": after})
        return send(
            ext[k].at[c, pl.ds(face, face)], ext[k].at[c, pl.ds(rows + face, face)], {"slab": before}
        )

    for layer in outer:
        send_tiles(layer)
    halos = {}
    for c in range(chunks):
        loads[c].wait()
        halos[0, c] = [send_halo(0, c, False), send_halo(0, c, True)]
    for layer in inner_layers:
        merge(layer)
        send_tiles(layer)

    def apply_layer(k, c, layer):
        product = jnp.dot(
            tiles[layer], ext[k][c, layer * face:(layer + 3) * face, :],
            preferred_element_type=jnp.float32,
        )
        inner = slice((layer + 1) * face, (layer + 2) * face)
        if k == 1 or k == 2:
            product = 2.0 * product - ext[k - 1][c, inner, :].astype(jnp.float32)
        if k < 3:
            ext[k + 1][c, inner, :] = product.astype(jnp.bfloat16)
        else:
            own_applied[c, layer * face:(layer + 1) * face, :] = product.astype(jnp.bfloat16)

    strip_copies = {}
    mine_at = pl.multiple_of(band * strip, strip)
    theirs_at = pl.multiple_of(other * strip, strip)

    def send_strip(c):
        strip_copies[4, c] = [send(
            own_applied.at[c, pl.ds(theirs_at, strip)], strip4.at[band * chunks + c], {"band": other}
        )]

    def send_part(c, source, place, size):
        strip_copies.setdefault((3, c), []).append(send(
            ext3.at[c, pl.ds(pl.multiple_of(face + source, face), size)],
            strip3.at[band * chunks + c, pl.ds(pl.multiple_of(place, face), size)],
            {"band": other},
        ))

    def send_inner(c):
        send_part(c, other * strip + band * face, band * face, strip - face)

    def send_outer(c):
        send_part(c, other * (rows - face), other * (strip - face), face)

    def keep_strip(which, c, source, base):
        place = strip3 if which == 3 else strip4
        place[band * chunks + c] = source[c, pl.ds(base + mine_at, strip), :]

    def outer_layer(k, c, layer):
        halos[k, c][1 if layer == 0 else 0].wait_recv()
        apply_layer(k, c, layer)
        if k < 3:
            halos.setdefault((k + 1, c), []).append(send_halo(k + 1, c, layer != 0))

    for layer in outer:
        place_tiles(layer)
        for c in range(chunks):
            outer_layer(0, c, layer)
    for layer in inner_layers:
        place_tiles(layer)
        for c in range(chunks):
            apply_layer(0, c, layer)
    for k in range(1, 4):
        for c in range(chunks):
            for layer in inner_layers:
                apply_layer(k, c, layer)
            if k == 2:
                send_inner(c)
        if k == 3:
            for c in range(chunks):
                slab_t[c] = ext3[c, face:face + rows, :].T
        for c in range(chunks):
            for layer in outer:
                outer_layer(k, c, layer)
            if k == 2:
                send_outer(c)
                keep_strip(3, c, ext3, face)
            if k == 3:
                if c < chunks - 1:
                    send_strip(c)
                keep_strip(4, c, own_applied, 0)

    def unit_start(unit, left, right):
        to_core[unit] = jnp.dot(
            left(1 - core), right, preferred_element_type=jnp.float32
        ).astype(jnp.bfloat16)
        copy = send(to_core.at[unit], from_core.at[unit], sibling)
        own32[unit] = jnp.dot(left(core), right, preferred_element_type=jnp.float32)
        return copy

    def unit_spread(unit, copy, place, first, plane):
        copy.wait_recv()
        to_peers[unit] = (own32[unit] + from_core[unit].astype(jnp.float32)).astype(jnp.bfloat16)
        copies = []
        for j in range(first, chips):
            target = ring(j)
            copies.append(send(
                to_peers.at[unit, pl.ds(pl.multiple_of(target * piece, piece), piece)],
                from_peers.at[place + j],
                at_chip(target, plane),
            ))
        return copies

    my_piece = pl.multiple_of(chip * piece, piece)

    def piece_sum(unit, places):
        total = to_peers[unit, pl.ds(my_piece, piece), :].astype(jnp.float32)
        for place in places:
            total = total + from_peers[place].astype(jnp.float32)
        return total

    def summed(unit, places, quad, c):
        total = piece_sum(unit, places)
        row = pl.multiple_of(core * width + my_piece, piece)
        gram16[quad * chunks + c, pl.ds(row, piece), :] = (total * gram_scale).astype(jnp.bfloat16)

    def pass_on(quad, index, device, span):
        row = pl.multiple_of(core * width + index * piece, piece)
        ref = gram16.at[pl.ds(quad * chunks + span[0], span[1]), pl.ds(row, piece)]
        return send(ref, ref, device)

    def place_of(c, kind):
        return (c * 3 + kind) * chips

    last = chunks - 1
    diag = [c for c in range(chunks)]
    near = [chunks + c for c in range(chunks)]
    cross = [2 * chunks + c for c in range(chunks)]

    starts = [
        unit_start(diag[c], lambda d: slab_t[d], own_applied[c])
        for c in range(chunks)
    ]
    diag_pieces = [
        unit_spread(diag[c], starts[c], place_of(c, 0), 1, band) for c in range(chunks)
    ]
    for c in range(chunks):
        for copy in strip_copies[3, c]:
            copy.wait_recv()
        other_t[c] = strip3[other * chunks + c].T
    starts = [
        unit_start(near[c], lambda d: other_t[d], strip4[band * chunks + c])
        for c in range(chunks)
    ]
    near_pieces = [
        unit_spread(near[c], starts[c], place_of(c, 1), 1, band) for c in range(chunks)
    ]

    def level_chip(offset):
        return lax.rem(level + offset, depth) * 2 + column

    beside = level * 2 + (1 - column)
    own_diag, other_diag = band * 3, other * 3
    own_off, other_off = other * 2 + band, band * 2 + other

    for c in range(chunks):
        for copy in diag_pieces[c]:
            copy.wait_recv()
        summed(diag[c], [place_of(c, 0) + j for j in range(1, chips)], own_diag, c)

    whole = (0, chunks)
    across = pass_on(own_diag, chip, at_chip(chip, other), whole)
    send_strip(last)
    diag_levels, diag_sides = [], []

    def spread_diag(quad):
        diag_sides.append(pass_on(quad, chip, at_chip(beside, band), whole))
        for j in range(1, depth):
            diag_levels.append((quad, j, pass_on(quad, chip, at_chip(level_chip(j), band), whole)))

    def block_to_sibling(quad, span):
        row = pl.multiple_of(core * width, width)
        ref = gram16.at[pl.ds(quad * chunks + span[0], span[1]), pl.ds(row, width)]
        return send(ref, ref, sibling)

    spread_diag(own_diag)

    def cross_unit(c, first, plane):
        for copy in strip_copies[4, c]:
            copy.wait_recv()
        start = unit_start(
            cross[c], lambda d: slab_t[d, :, pl.ds(mine_at, strip)], strip4[other * chunks + c]
        )
        return unit_spread(cross[c], start, place_of(c, 2), first, plane)

    cross_copies = {c: cross_unit(c, 1, band) for c in range(last)}
    across.wait_recv()
    spread_diag(other_diag)
    for c in range(last):
        for copy in cross_copies[c]:
            copy.wait_recv()
        total = piece_sum(cross[c], [place_of(c, 2) + j for j in range(1, chips)])
        crossing[c] = total.astype(jnp.bfloat16)
        cross_copies[c] = [send(crossing.at[c], from_peers.at[place_of(c, 2)], at_chip(chip, other))]
    for quad, j, copy in diag_levels:
        copy.wait_recv()
        diag_sides.append(pass_on(quad, level_chip(depth - j), at_chip(beside, band), whole))
    cross_copies[last] = cross_unit(last, 0, other)
    for copy in diag_sides:
        copy.wait_recv()
    early_copies = [block_to_sibling(quad, whole) for quad in (own_diag, other_diag)]

    def sum_off(c):
        for copy in near_pieces[c] + cross_copies[c]:
            copy.wait_recv()
        places = [place_of(c, 1) + j for j in range(1, chips)]
        places += [place_of(c, 2) + j for j in range(chips if c == last else 1)]
        summed(near[c], places, own_off, c)

    def spread_plane(index, span):
        return [
            pass_on(own_off, index, at_chip(chip, other), span),
            pass_on(own_off, index, at_chip(beside, band), span),
            pass_on(own_off, index, at_chip(beside, other), span),
        ]

    plane_copies = {}
    for c in range(chunks):
        sum_off(c)
        span = (c, 1)
        level_copies = [
            (j, pass_on(own_off, chip, at_chip(level_chip(j), band), span))
            for j in range(1, depth)
        ]
        plane_copies[c] = spread_plane(chip, span)
        for j, copy in level_copies:
            copy.wait_recv()
            plane_copies[c] += spread_plane(level_chip(depth - j), span)

    def mix(gr, gc, c):
        left = jnp.concatenate([strip3[gr * chunks + d] for d in range(chunks)], axis=1)
        return jnp.dot(
            left, gram16[(gr * 2 + gc) * chunks + c], preferred_element_type=jnp.float32
        )

    for copy in early_copies:
        copy.wait_recv()
    for gc in range(2):
        for c in range(chunks):
            q = gc * chunks + c
            out32[q] = strip4[q].astype(jnp.float32) - mix(gc, gc, c)
    core_copies = {}
    for c in range(chunks):
        for copy in plane_copies[c]:
            copy.wait_recv()
        core_copies[c] = [block_to_sibling(quad, (c, 1)) for quad in (own_off, other_off)]
    for c in range(chunks):
        for copy in core_copies[c]:
            copy.wait_recv()
        for gc in range(2):
            q = gc * chunks + c
            out_ref[:, q * width:(q + 1) * width] = (out32[q] - mix(1 - gc, gc, c)).astype(
                jnp.bfloat16
            )
    assert len(sent) <= send_sem.shape[0]
    for copy in sent:
        copy.wait_send()


def fused_body(slabs, hamiltonian, neighbors, orbitals):
    blocks, slots, part, tile = hamiltonian.shape
    rows, bands = orbitals.shape
    layers = blocks // FACE
    width = bands // CHUNKS
    groups = 2 * CHUNKS
    strip = rows // 2
    face = FACE * tile
    chips, depth = slabs // 2, slabs // 4
    piece = width // chips
    units = 3 * CHUNKS
    gram_scale = 1.0 / math.sqrt(float(rows * slabs) * float(bands * 2))
    copies = layers + 8 * CHUNKS + 3 * CHUNKS + units * (chips + 1) + 4 * depth + 5
    copies += CHUNKS * (4 * depth + 4)
    half = jnp.bfloat16
    flops = 2 * rows * 6 * tile * bands * 4 + 2 * 2 * strip * 4 * bands * bands
    return pl.pallas_call(
        functools.partial(kernel, slabs, gram_scale),
        out_shape=jax.ShapeDtypeStruct((strip, 2 * bands), half),
        in_specs=[
            pl.BlockSpec(memory_space=pltpu.HBM),
            pl.BlockSpec(memory_space=pltpu.HBM),
            pl.BlockSpec(memory_space=pltpu.HBM),
        ],
        out_specs=pl.BlockSpec(memory_space=pltpu.VMEM),
        scratch_shapes=[
            pltpu.SMEM((blocks, slots), jnp.int32),
            pltpu.VMEM((blocks, slots, part, tile), half),
            pltpu.VMEM((layers, FACE, part, 4 * tile), half),
            pltpu.VMEM((layers, FACE, part, 4 * tile), half),
            pltpu.VMEM((layers, face, 3 * face), half),
            pltpu.VMEM((CHUNKS, width, rows), half),
            pltpu.VMEM((CHUNKS, width, strip), half),
            *[pltpu.VMEM((CHUNKS, rows + 2 * face, width), half) for _ in range(4)],
            pltpu.VMEM((CHUNKS, rows, width), half),
            pltpu.VMEM((groups, strip, width), half),
            pltpu.VMEM((groups, strip, width), half),
            pltpu.VMEM((units, width, width), jnp.float32),
            pltpu.VMEM((units, width, width), half),
            pltpu.VMEM((units, width, width), half),
            pltpu.VMEM((units, width, width), half),
            pltpu.VMEM((units * chips, piece, width), half),
            pltpu.VMEM((CHUNKS, piece, width), half),
            pltpu.VMEM((4 * CHUNKS, CHUNKS * width, width), half),
            pltpu.VMEM((groups, strip, width), jnp.float32),
            pltpu.SemaphoreType.DMA((CHUNKS + layers + 1,)),
            pltpu.SemaphoreType.DMA((copies,)),
            pltpu.SemaphoreType.DMA((copies,)),
        ],
        compiler_params=pltpu.CompilerParams(
            collective_id=0, has_side_effects=True, vmem_limit_bytes=62 * 1024 * 1024 + 768 * 1024
        ),
        cost_estimate=pl.CostEstimate(flops=flops, bytes_accessed=4 * rows * bands, transcendentals=0),
    )(neighbors, hamiltonian, orbitals)


def solution(mesh):
    in_specs = (P("slab", None, "band", None), P("slab", None), P("slab", "band"))
    out_specs = P(("slab", "band"), None)
    slabs, groups = mesh.shape["slab"], mesh.shape["band"]
    pairs = groups == 2 and slabs >= 8 and slabs % 4 == 0 and CHUNKS == 2
    body = functools.partial(fused_body, slabs) if pairs else plain_body
    return jax.shard_map(body, mesh=mesh, in_specs=in_specs, out_specs=out_specs, check_vma=False)
```

```python
import functools
import math

import jax
import jax.numpy as jnp
from jax import lax
from jax.experimental import pallas as pl
from jax.experimental.pallas import tpu as pltpu
from jax.sharding import PartitionSpec as P

FACE = 2
CHUNKS = 2
MESH = pl.DeviceIdType.MESH


def padded(block, sides, width):
    for axis, dim in sides:
        count = lax.axis_size(axis)
        forward = [(i, i + 1) for i in range(count - 1)]
        forward.append((count - 1, 0))
        backward = [(target, source) for source, target in forward]
        low = lax.ppermute(
            lax.slice_in_dim(block, block.shape[dim] - width, None, axis=dim), axis, forward
        )
        high = lax.ppermute(lax.slice_in_dim(block, 0, width, axis=dim), axis, backward)
        block = jnp.concatenate([low, block, high], axis=dim)
    return block


def apply_local(vector, full_tiles, neighbors):
    tile_size = full_tiles.shape[2]
    extended = padded(vector, (("slab", 0),), FACE * tile_size)
    blocks = extended.reshape(-1, tile_size, vector.shape[1])
    picked_blocks = blocks[neighbors]
    product = jnp.einsum(
        "rjab,rjbc->rac", full_tiles, picked_blocks, preferred_element_type=jnp.float32
    )
    return product.reshape(vector.shape[0], vector.shape[1])


def plain_body(hamiltonian, neighbors, orbitals):
    full_tiles = lax.all_gather(hamiltonian, "band", axis=2, tiled=True)
    first = apply_local(orbitals, full_tiles, neighbors).astype(jnp.bfloat16)
    second = (
        2.0 * apply_local(first, full_tiles, neighbors) - orbitals.astype(jnp.float32)
    ).astype(jnp.bfloat16)
    third = (2.0 * apply_local(second, full_tiles, neighbors) - first.astype(jnp.float32)).astype(
        jnp.bfloat16
    )
    applied = apply_local(third, full_tiles, neighbors).astype(jnp.bfloat16)
    rows_all = orbitals.shape[0] * lax.axis_size("slab")
    bands_all = orbitals.shape[1] * lax.axis_size("band")
    gram_scale = 1.0 / math.sqrt(float(rows_all) * float(bands_all))
    strip_third, strip_applied = (
        lax.all_to_all(third, "band", split_axis=0, concat_axis=1, tiled=True),
        lax.all_to_all(applied, "band", split_axis=0, concat_axis=1, tiled=True),
    )
    row_block = lax.psum_scatter(
        jnp.einsum(
            "rb,rc->bc", strip_third, strip_applied, preferred_element_type=jnp.float32
        ).astype(jnp.bfloat16),
        "band",
        scatter_dimension=0,
        tiled=True,
    ).astype(jnp.float32)
    slab_summed = lax.psum(row_block, "slab")
    gram_block = (slab_summed * gram_scale).astype(jnp.bfloat16)
    mixed = jnp.dot(
        strip_third,
        lax.all_gather(gram_block, "band", axis=0, tiled=True),
        preferred_element_type=jnp.float32,
    )
    return (strip_applied.astype(jnp.float32) - mixed).astype(jnp.bfloat16)


def kernel(
    slabs, gram_scale, neighbors_ref, hamiltonian_ref, orbitals_ref, out_ref,
    names, slots, pieces, arrived, tiles, slab_t, other_t, ext0, ext1, ext2, ext3, own_applied, strip3, strip4, own32, to_core, from_core,
    to_peers, from_peers, to_side, from_side, to_level, crossing, gram16, out32, local_sem, send_sem, recv_sem,
):
    slab, band = lax.axis_index("slab"), lax.axis_index("band")
    other = 1 - band
    after, before = lax.rem(slab + 1, slabs), lax.rem(slab + slabs - 1, slabs)
    blocks, _, part, _ = slots.shape
    tile = 2 * part
    layers = blocks // FACE
    face = FACE * tile
    rows = blocks * tile
    chunks, _, width = ext0.shape
    strip = rows // 2
    groups = 2 * chunks
    ext = [ext0, ext1, ext2, ext3]

    chips, depth = slabs // 2, slabs // 4
    core, chip = lax.rem(slab, 2), lax.div(slab, 2)
    column, level = lax.rem(chip, 2), lax.div(chip, 2)
    sibling = {"slab": chip * 2 + (1 - core)}
    piece = width // chips

    def at_chip(index, plane):
        return {"slab": index * 2 + core, "band": plane}

    def ring(offset):
        return lax.rem(chip + offset, chips)

    barrier = pltpu.get_barrier_semaphore()
    greeted = [{"slab": after}, {"slab": before}, sibling]
    greeted += [at_chip(ring(j), band) for j in range(1, chips)]
    greeted += [at_chip(ring(j), other) for j in range(chips)]

    outer = [0, layers - 1]
    inner_layers = list(range(1, layers - 1))
    order = outer + inner_layers
    name_load = pltpu.make_async_copy(neighbors_ref, names, local_sem.at[chunks + layers])
    name_load.start()
    tile_loads = {}
    for layer in order:
        span = pl.ds(layer * FACE, FACE)
        tile_loads[layer] = pltpu.make_async_copy(
            hamiltonian_ref.at[span], slots.at[span], local_sem.at[chunks + layer]
        )
        tile_loads[layer].start()
    loads = []
    for c in range(chunks):
        load = pltpu.make_async_copy(
            orbitals_ref.at[:, pl.ds(c * width, width)],
            ext0.at[c, pl.ds(face, rows)],
            local_sem.at[c],
        )
        load.start()
        loads.append(load)
    for target in greeted:
        pl.semaphore_signal(barrier, inc=1, device_id=target, device_id_type=MESH)

    def spans(a):
        if a == 0:
            return ((0, 0, tile), (tile, 2 * tile, 3 * tile))
        return ((0, tile, 3 * tile), (3 * tile, 5 * tile, tile))

    def put(layer, a, side, merged):
        row = pl.multiple_of(a * tile + side * part, part)
        for start, place, size in spans(a):
            tiles[layer, pl.ds(row, part), place:place + size] = merged[:, start:start + size]

    def merge(layer):
        tile_loads[layer].wait()
        for a in range(FACE):
            row = layer * FACE + a
            sources = (row, FACE + layer * FACE, FACE + layer * FACE + 1, row + 2 * FACE)
            totals = [jnp.zeros((part, tile), jnp.float32) for _ in sources]
            for slot in range(slots.shape[1]):
                name = names[row, slot]
                entry = slots[row, slot].astype(jnp.float32)
                for n, source in enumerate(sources):
                    totals[n] = totals[n] + jnp.where(name == source, entry, 0.0)
            merged = jnp.concatenate([total.astype(jnp.bfloat16) for total in totals], axis=1)
            pieces[layer, a] = merged
            put(layer, a, band, merged)
            hole = (tile, 5 * tile) if a == 0 else (0, 4 * tile)
            for place in hole:
                tiles[layer, a * tile:(a + 1) * tile, place:place + tile] = jnp.zeros(
                    (tile, tile), jnp.bfloat16
                )

    name_load.wait()
    for layer in outer:
        merge(layer)
    pl.semaphore_wait(barrier, len(greeted))

    sent = []

    def send(source, target, device):
        n = len(sent)
        copy = pltpu.make_async_remote_copy(
            src_ref=source, dst_ref=target, send_sem=send_sem.at[n], recv_sem=recv_sem.at[n],
            device_id=device, device_id_type=MESH,
        )
        copy.start()
        sent.append(copy)
        return copy

    tile_copies = {}

    def send_tiles(layer):
        tile_copies[layer] = send(pieces.at[layer], arrived.at[layer], {"band": other})

    def place_tiles(layer):
        tile_copies[layer].wait_recv()
        for a in range(FACE):
            put(layer, a, other, arrived[layer, a])

    def send_halo(k, c, up):
        if up:
            return send(ext[k].at[c, pl.ds(rows, face)], ext[k].at[c, pl.ds(0, face)], {"slab": after})
        return send(
            ext[k].at[c, pl.ds(face, face)], ext[k].at[c, pl.ds(rows + face, face)], {"slab": before}
        )

    for layer in outer:
        send_tiles(layer)
    halos = {}
    for c in range(chunks):
        loads[c].wait()
        halos[0, c] = [send_halo(0, c, False), send_halo(0, c, True)]
    for layer in inner_layers:
        merge(layer)
        send_tiles(layer)

    def apply_layer(k, c, layer):
        product = jnp.dot(
            tiles[layer], ext[k][c, layer * face:(layer + 3) * face, :],
            preferred_element_type=jnp.float32,
        )
        inner = slice((layer + 1) * face, (layer + 2) * face)
        if k == 1 or k == 2:
            product = 2.0 * product - ext[k - 1][c, inner, :].astype(jnp.float32)
        if k < 3:
            ext[k + 1][c, inner, :] = product.astype(jnp.bfloat16)
        else:
            own_applied[c, layer * face:(layer + 1) * face, :] = product.astype(jnp.bfloat16)

    strip_copies = {}
    mine_at = pl.multiple_of(band * strip, strip)
    theirs_at = pl.multiple_of(other * strip, strip)

    def send_strip(c):
        strip_copies[4, c] = [send(
            own_applied.at[c, pl.ds(theirs_at, strip)], strip4.at[band * chunks + c], {"band": other}
        )]

    def send_part(c, source, place, size):
        strip_copies.setdefault((3, c), []).append(send(
            ext3.at[c, pl.ds(pl.multiple_of(face + source, face), size)],
            strip3.at[band * chunks + c, pl.ds(pl.multiple_of(place, face), size)],
            {"band": other},
        ))

    def send_inner(c):
        send_part(c, other * strip + band * face, band * face, strip - face)

    def send_outer(c):
        send_part(c, other * (rows - face), other * (strip - face), face)

    def keep_strip(which, c, source, base):
        place = strip3 if which == 3 else strip4
        place[band * chunks + c] = source[c, pl.ds(base + mine_at, strip), :]

    def outer_layer(k, c, layer):
        halos[k, c][1 if layer == 0 else 0].wait_recv()
        apply_layer(k, c, layer)
        if k < 3:
            halos.setdefault((k + 1, c), []).append(send_halo(k + 1, c, layer != 0))

    for layer in outer:
        place_tiles(layer)
        for c in range(chunks):
            outer_layer(0, c, layer)
    for layer in inner_layers:
        place_tiles(layer)
        for c in range(chunks):
            apply_layer(0, c, layer)
    for k in range(1, 4):
        for c in range(chunks):
            for layer in inner_layers:
                apply_layer(k, c, layer)
            if k == 2:
                send_inner(c)
        if k == 3:
            for c in range(chunks):
                slab_t[c] = ext3[c, face:face + rows, :].T
        for c in range(chunks):
            for layer in outer:
                outer_layer(k, c, layer)
            if k == 2:
                send_outer(c)
                keep_strip(3, c, ext3, face)
            if k == 3:
                if c < chunks - 1:
                    send_strip(c)
                keep_strip(4, c, own_applied, 0)

    def unit_start(unit, left, right):
        to_core[unit] = jnp.dot(
            left(1 - core), right, preferred_element_type=jnp.float32
        ).astype(jnp.bfloat16)
        copy = send(to_core.at[unit], from_core.at[unit], sibling)
        own32[unit] = jnp.dot(left(core), right, preferred_element_type=jnp.float32)
        return copy

    def unit_spread(unit, copy, place, first, plane):
        copy.wait_recv()
        to_peers[unit] = (own32[unit] + from_core[unit].astype(jnp.float32)).astype(jnp.bfloat16)
        copies = []
        for j in range(first, chips):
            target = ring(j)
            copies.append(send(
                to_peers.at[unit, pl.ds(pl.multiple_of(target * piece, piece), piece)],
                from_peers.at[place + j],
                at_chip(target, plane),
            ))
        return copies

    beside = level * 2 + (1 - column)

    def level_chip(offset):
        return lax.rem(level + offset, depth) * 2 + column

    def side_start(unit, copy):
        copy.wait_recv()
        own32[unit] = own32[unit] + from_core[unit].astype(jnp.float32)
        for z in range(depth):
            row = pl.multiple_of((z * 2 + 1 - column) * piece, piece)
            to_side[unit, z] = own32[unit, pl.ds(row, piece), :].astype(jnp.bfloat16)
        return send(to_side.at[unit], from_side.at[unit], at_chip(beside, band))

    def level_start(unit, copy, place):
        copy.wait_recv()
        for z in range(depth):
            row = pl.multiple_of((z * 2 + column) * piece, piece)
            to_level[unit, z] = (
                own32[unit, pl.ds(row, piece), :] + from_side[unit, z].astype(jnp.float32)
            ).astype(jnp.bfloat16)
        return [
            send(
                to_level.at[unit, lax.rem(level + j, depth)],
                from_peers.at[place + j],
                at_chip(level_chip(j), band),
            )
            for j in range(1, depth)
        ]

    my_piece = pl.multiple_of(chip * piece, piece)

    def piece_sum(unit, places):
        total = to_level[unit, level].astype(jnp.float32)
        for place in places:
            total = total + from_peers[place].astype(jnp.float32)
        return total

    def summed(unit, places, quad, c):
        total = piece_sum(unit, places)
        row = pl.multiple_of(core * width + my_piece, piece)
        gram16[quad * chunks + c, pl.ds(row, piece), :] = (total * gram_scale).astype(jnp.bfloat16)

    def pass_on(quad, index, device, span):
        row = pl.multiple_of(core * width + index * piece, piece)
        ref = gram16.at[pl.ds(quad * chunks + span[0], span[1]), pl.ds(row, piece)]
        return send(ref, ref, device)

    def place_of(c, kind):
        return (c * 3 + kind) * chips

    last = chunks - 1
    diag = [c for c in range(chunks)]
    near = [chunks + c for c in range(chunks)]
    cross = [2 * chunks + c for c in range(chunks)]

    starts = [
        unit_start(diag[c], lambda d: slab_t[d], own_applied[c])
        for c in range(chunks)
    ]
    sides = [side_start(diag[c], starts[c]) for c in range(chunks)]
    diag_pieces = [level_start(diag[c], sides[c], place_of(c, 0)) for c in range(chunks)]
    for c in range(chunks):
        for copy in strip_copies[3, c]:
            copy.wait_recv()
        other_t[c] = strip3[other * chunks + c].T
    starts = [
        unit_start(near[c], lambda d: other_t[d], strip4[band * chunks + c])
        for c in range(chunks)
    ]
    sides = [side_start(near[c], starts[c]) for c in range(chunks)]
    near_pieces = [level_start(near[c], sides[c], place_of(c, 1)) for c in range(chunks)]

    own_diag, other_diag = band * 3, other * 3
    own_off, other_off = other * 2 + band, band * 2 + other

    for c in range(chunks):
        for copy in diag_pieces[c]:
            copy.wait_recv()
        summed(diag[c], [place_of(c, 0) + j for j in range(1, depth)], own_diag, c)

    whole = (0, chunks)
    across = pass_on(own_diag, chip, at_chip(chip, other), whole)
    send_strip(last)
    diag_levels, diag_sides = [], []

    def spread_diag(quad):
        diag_sides.append(pass_on(quad, chip, at_chip(beside, band), whole))
        for j in range(1, depth):
            diag_levels.append((quad, j, pass_on(quad, chip, at_chip(level_chip(j), band), whole)))

    def block_to_sibling(quad, span):
        row = pl.multiple_of(core * width, width)
        ref = gram16.at[pl.ds(quad * chunks + span[0], span[1]), pl.ds(row, width)]
        return send(ref, ref, sibling)

    spread_diag(own_diag)

    def cross_start(c):
        for copy in strip_copies[4, c]:
            copy.wait_recv()
        return unit_start(
            cross[c], lambda d: slab_t[d, :, pl.ds(mine_at, strip)], strip4[other * chunks + c]
        )

    cross_copies = {}
    for c in range(last):
        side = side_start(cross[c], cross_start(c))
        cross_copies[c] = level_start(cross[c], side, place_of(c, 2))
    across.wait_recv()
    spread_diag(other_diag)
    for c in range(last):
        for copy in cross_copies[c]:
            copy.wait_recv()
        total = piece_sum(cross[c], [place_of(c, 2) + j for j in range(1, depth)])
        crossing[c] = total.astype(jnp.bfloat16)
        cross_copies[c] = [send(crossing.at[c], from_peers.at[place_of(c, 2)], at_chip(chip, other))]
    for quad, j, copy in diag_levels:
        copy.wait_recv()
        diag_sides.append(pass_on(quad, level_chip(depth - j), at_chip(beside, band), whole))
    cross_copies[last] = unit_spread(cross[last], cross_start(last), place_of(last, 2), 0, other)
    for copy in diag_sides:
        copy.wait_recv()
    early_copies = [block_to_sibling(quad, whole) for quad in (own_diag, other_diag)]

    def sum_off(c):
        for copy in near_pieces[c] + cross_copies[c]:
            copy.wait_recv()
        places = [place_of(c, 1) + j for j in range(1, depth)]
        places += [place_of(c, 2) + j for j in range(chips if c == last else 1)]
        summed(near[c], places, own_off, c)

    def spread_plane(index, span):
        return [
            pass_on(own_off, index, at_chip(chip, other), span),
            pass_on(own_off, index, at_chip(beside, band), span),
            pass_on(own_off, index, at_chip(beside, other), span),
        ]

    plane_copies = {}
    for c in range(chunks):
        sum_off(c)
        span = (c, 1)
        level_copies = [
            (j, pass_on(own_off, chip, at_chip(level_chip(j), band), span))
            for j in range(1, depth)
        ]
        plane_copies[c] = spread_plane(chip, span)
        for j, copy in level_copies:
            copy.wait_recv()
            plane_copies[c] += spread_plane(level_chip(depth - j), span)

    def mix(gr, gc, c):
        left = jnp.concatenate([strip3[gr * chunks + d] for d in range(chunks)], axis=1)
        return jnp.dot(
            left, gram16[(gr * 2 + gc) * chunks + c], preferred_element_type=jnp.float32
        )

    for copy in early_copies:
        copy.wait_recv()
    for gc in range(2):
        for c in range(chunks):
            q = gc * chunks + c
            out32[q] = strip4[q].astype(jnp.float32) - mix(gc, gc, c)
    core_copies = {}
    for c in range(chunks):
        for copy in plane_copies[c]:
            copy.wait_recv()
        core_copies[c] = [block_to_sibling(quad, (c, 1)) for quad in (own_off, other_off)]
    for c in range(chunks):
        for copy in core_copies[c]:
            copy.wait_recv()
        for gc in range(2):
            q = gc * chunks + c
            out_ref[:, q * width:(q + 1) * width] = (out32[q] - mix(1 - gc, gc, c)).astype(
                jnp.bfloat16
            )
    assert len(sent) <= send_sem.shape[0]
    for copy in sent:
        copy.wait_send()


def fused_body(slabs, hamiltonian, neighbors, orbitals):
    blocks, slots, part, tile = hamiltonian.shape
    rows, bands = orbitals.shape
    layers = blocks // FACE
    width = bands // CHUNKS
    groups = 2 * CHUNKS
    strip = rows // 2
    face = FACE * tile
    chips, depth = slabs // 2, slabs // 4
    piece = width // chips
    units = 3 * CHUNKS
    gram_scale = 1.0 / math.sqrt(float(rows * slabs) * float(bands * 2))
    copies = layers + 8 * CHUNKS + 3 * CHUNKS + units * (chips + 1) + 4 * depth + 5
    copies += CHUNKS * (4 * depth + 4)
    half = jnp.bfloat16
    flops = 2 * rows * 6 * tile * bands * 4 + 2 * 2 * strip * 4 * bands * bands
    return pl.pallas_call(
        functools.partial(kernel, slabs, gram_scale),
        out_shape=jax.ShapeDtypeStruct((strip, 2 * bands), half),
        in_specs=[
            pl.BlockSpec(memory_space=pltpu.HBM),
            pl.BlockSpec(memory_space=pltpu.HBM),
            pl.BlockSpec(memory_space=pltpu.HBM),
        ],
        out_specs=pl.BlockSpec(memory_space=pltpu.VMEM),
        scratch_shapes=[
            pltpu.SMEM((blocks, slots), jnp.int32),
            pltpu.VMEM((blocks, slots, part, tile), half),
            pltpu.VMEM((layers, FACE, part, 4 * tile), half),
            pltpu.VMEM((layers, FACE, part, 4 * tile), half),
            pltpu.VMEM((layers, face, 3 * face), half),
            pltpu.VMEM((CHUNKS, width, rows), half),
            pltpu.VMEM((CHUNKS, width, strip), half),
            *[pltpu.VMEM((CHUNKS, rows + 2 * face, width), half) for _ in range(4)],
            pltpu.VMEM((CHUNKS, rows, width), half),
            pltpu.VMEM((groups, strip, width), half),
            pltpu.VMEM((groups, strip, width), half),
            pltpu.VMEM((units, width, width), jnp.float32),
            pltpu.VMEM((units, width, width), half),
            pltpu.VMEM((units, width, width), half),
            pltpu.VMEM((units, width, width), half),
            pltpu.VMEM((units * chips, piece, width), half),
            *[pltpu.VMEM((units, depth, piece, width), half) for _ in range(3)],
            pltpu.VMEM((CHUNKS, piece, width), half),
            pltpu.VMEM((4 * CHUNKS, CHUNKS * width, width), half),
            pltpu.VMEM((groups, strip, width), jnp.float32),
            pltpu.SemaphoreType.DMA((CHUNKS + layers + 1,)),
            pltpu.SemaphoreType.DMA((copies,)),
            pltpu.SemaphoreType.DMA((copies,)),
        ],
        compiler_params=pltpu.CompilerParams(
            collective_id=0, has_side_effects=True, vmem_limit_bytes=62 * 1024 * 1024 + 768 * 1024
        ),
        cost_estimate=pl.CostEstimate(flops=flops, bytes_accessed=4 * rows * bands, transcendentals=0),
    )(neighbors, hamiltonian, orbitals)


def solution(mesh):
    in_specs = (P("slab", None, "band", None), P("slab", None), P("slab", "band"))
    out_specs = P(("slab", "band"), None)
    slabs, groups = mesh.shape["slab"], mesh.shape["band"]
    pairs = groups == 2 and slabs >= 8 and slabs % 4 == 0 and CHUNKS == 2
    body = functools.partial(fused_body, slabs) if pairs else plain_body
    return jax.shard_map(body, mesh=mesh, in_specs=in_specs, out_specs=out_specs, check_vma=False)
```
